256 devices in a mesh: depth: 8 (over x, y_lo), tile: 32 (over y_hi, z, core).
Axes of the slice: x: 4, y: 4 (y_hi: 2, y_lo: 2; y = y_hi * 2 + y_lo), z: 8, core: 2. Of those that a mesh axis runs over, the one named last changes fastest.
Arguments:
- scene_layers: bfloat16 [8, 4096, 256], P('depth', 'tile'), may hold values from -6 to 6
- sensor_grad: bfloat16 [4096, 256], P('tile'), may hold values from -0.0059814453 to 0.0059814453
- pupil_phase: float32 [1024, 1024], P('tile', 'depth'), may hold values from -3.140625 to 3.140625
- defocus_index: int32 [8], P('depth'), may hold values from -6 to 6
Outputs:
- phase_grad: float32 [1024, 1024], P('tile', 'depth')
The draws below stay inside these ranges and needn't reach their ends.
All inputs are finite; a program needn't handle non-finite values.
Results may differ from the reference program's by a relative error of at most 0.0003.
Values may be sent and summed in bfloat16 or wider, within the bound.
No kernel may reach another device: no remote copies, remote signals or barrier semaphores. Data moves between devices by JAX's collectives and lax.ppermute only.
A program may use at most 64 MiB of HBM per device.

```python
import jax
import jax.numpy as jnp
from jax import lax

PUPIL = 1024
HALF = 128
PSF = 256
COLS = 256
LAYERS = 8
SENSOR_ROWS = 4096


def plant(result, key, least, top_value):
    longest = result.shape.index(max(result.shape))
    spots = []
    for shift in (0, 1):
        where = [jax.random.randint(jax.random.fold_in(key, axis), (), 0, length) for axis, length in enumerate(result.shape)]
        where[longest] = (where[longest] + shift) % result.shape[longest]
        spots.append(tuple(where))
    return result.at[spots[0]].set(least).at[spots[1]].set(top_value)


def block_scale(stream_key, extent, shards, low, largest):
    def one(dim, shards_of):
        steps = jax.random.uniform(jax.random.fold_in(jax.random.fold_in(stream_key, 6), dim), (shards_of,), jnp.float32, low / len(shards), largest / len(shards))
        return jnp.repeat(jnp.exp(steps), extent[dim] // shards_of).reshape((-1,) + (1,) * (len(extent) - dim - 1))

    gain = one(*shards[0])
    for cut in shards[1:]:
        gain = gain * one(*cut)
    return gain


def normal_values(stream_key, dims, scale, most, split=(), kind=jnp.bfloat16):
    factor_of = block_scale(stream_key, dims, split, -0.22, 0.18) if split else 1.0
    drawn = jax.random.normal(stream_key, dims, jnp.float32) * scale * factor_of
    return jnp.minimum(jnp.maximum(drawn, -most), most).astype(kind)


def setup_inputs(seed: int = 0) -> dict:
    streams_of = jax.random.split(jax.random.key(seed), 5)
    scene_layers = normal_values(streams_of[0], (LAYERS, SENSOR_ROWS, COLS), 1.0, 6.0, ((0, 8), (1, 32)))
    sensor_grad = normal_values(streams_of[1], (SENSOR_ROWS, COLS), 0.001, 0.0059814453, ((0, 32),))
    pupil_phase = jnp.clip(jax.random.uniform(streams_of[2], (PUPIL, PUPIL), jnp.float32, -3.140625, 3.140625), -3.140625, 3.140625)
    defocus_index = plant(jax.random.randint(streams_of[3], (LAYERS,), -6, 7), jax.random.fold_in(streams_of[3], 1), -6, 6).astype(jnp.int32)
    return {"scene_layers": scene_layers, "sensor_grad": sensor_grad, "pupil_phase": pupil_phase, "defocus_index": defocus_index}


two_pi = 6.283185307179586
defocus_step = 0.5


def freq_tables(first_row, row_count, pupil_size, half_width):
    wave_index = (jnp.arange(2 * half_width, dtype=jnp.int32) - half_width)[:, None]
    pupil_index = (jnp.arange(row_count, dtype=jnp.int32) + first_row).astype(jnp.int32)[None, :]
    phase_angle = jnp.mod(wave_index * pupil_index, pupil_size).astype(jnp.float32) * (two_pi / pupil_size)
    unit_scale = pupil_size ** -0.5
    return jnp.cos(phase_angle) * unit_scale, -jnp.sin(phase_angle) * unit_scale


def pupil_terms(first_row, row_count, pupil_size):
    pupil_rows = (jnp.arange(row_count, dtype=jnp.int32) + first_row).astype(jnp.float32)[:, None]
    pupil_cols = jnp.arange(pupil_size, dtype=jnp.int32).astype(jnp.float32)[None, :]
    centre = (pupil_size - 1) / 2.0
    radius = (pupil_rows - centre) ** 2 + (pupil_cols - centre) ** 2
    limit = (pupil_size / 2.0) ** 2
    inside = (radius <= limit).astype(jnp.float32)
    return inside, radius / limit


def highest(left, right):
    return jnp.dot(left, right, precision=lax.Precision.HIGHEST)


def reference(scene_layers, sensor_grad, pupil_phase, defocus_index):
    total_rows = sensor_grad.shape[0]
    padded_rows = total_rows + 2 * HALF
    padded_cols = COLS + 2 * HALF
    grad_freq = jnp.fft.rfft2(jnp.pad(sensor_grad.astype(jnp.float32), ((0, 2 * HALF), (0, 2 * HALF))))
    row_cos, row_sin = freq_tables(0, PUPIL, PUPIL, HALF)
    inside, defocus_map = pupil_terms(0, PUPIL, PUPIL)
    phase_total = jnp.zeros((PUPIL, PUPIL), jnp.float32)
    for layer_pos in range(LAYERS):
        padded_scene = jnp.pad(scene_layers[layer_pos].astype(jnp.float32), ((HALF, HALF), (HALF, HALF)))
        product = jnp.fft.rfft2(padded_scene) * jnp.conj(grad_freq)
        kernel_grad = jnp.fft.irfft2(product, s=(padded_rows, padded_cols))[:PSF, :PSF].astype(jnp.float32)
        theta = pupil_phase + defocus_index[layer_pos].astype(jnp.float32) * defocus_step * defocus_map
        field_re = inside * jnp.cos(theta)
        field_im = inside * jnp.sin(theta)
        z_re = highest(field_re, row_cos.T) - highest(field_im, row_sin.T)
        z_im = highest(field_re, row_sin.T) + highest(field_im, row_cos.T)
        y_re = highest(row_cos, z_re) - highest(row_sin, z_im)
        y_im = highest(row_cos, z_im) + highest(row_sin, z_re)
        gy_re = 2.0 * kernel_grad * y_re
        gy_im = 2.0 * kernel_grad * y_im
        gz_re = highest(row_cos.T, gy_re) + highest(row_sin.T, gy_im)
        gz_im = highest(row_cos.T, gy_im) - highest(row_sin.T, gy_re)
        ge_re = highest(gz_re, row_cos) + highest(gz_im, row_sin)
        ge_im = highest(gz_im, row_cos) - highest(gz_re, row_sin)
        phase_total = phase_total + field_re * ge_im - field_im * ge_re
    return phase_total
```

```python
import numpy as np
import jax
import jax.numpy as jnp
import ml_dtypes
from jax import lax
from jax.experimental import pallas as pl
from jax.experimental.pallas import tpu as pltpu
from jax.sharding import PartitionSpec as P

PUPIL = 1024
HALF = 128
FREQ = 2 * HALF
GROUP = 16
GATHER_MASKS = (0, 2, 1, 3, 6, 4, 7, 5)
EVEN, ODD = (0, 2, 4, 6), (1, 3, 5, 7)
WINDOW = FREQ + GROUP
defocus_step = 0.5


def split_table(table):
    high = table.astype(ml_dtypes.bfloat16)
    return high, (table - high.astype(np.float64)).astype(ml_dtypes.bfloat16)


def freq_tables():
    waves = np.arange(FREQ, dtype=np.int64) - HALF
    angle = (waves[:, None] * np.arange(PUPIL)[None, :]) % PUPIL * (2 * np.pi / PUPIL)
    cos, sin = np.cos(angle) * PUPIL**-0.5, -np.sin(angle) * PUPIL**-0.5
    gather = split_table(np.concatenate([cos.T, sin.T], axis=1))
    spread = split_table(np.concatenate([cos, sin], axis=1))
    half, chip, core, row = np.indices((2, FREQ // GROUP, 2, 4)).reshape(4, -1)
    arrived = 128 * core + 8 * chip + 4 * half + row
    return gather, spread, [part[arrived] for part in spread]


def split(x):
    high = x.astype(jnp.bfloat16)
    return high, (x - high.astype(jnp.float32)).astype(jnp.bfloat16)


def dot(left, right):
    return jnp.dot(left, right, preferred_element_type=jnp.float32)


def dot3(left, high_ref, low_ref):
    rows = left.shape[0]
    high, low = split(left)
    both = dot(jnp.concatenate([high, low], axis=0), high_ref[...])
    return both[:rows] + both[rows:] + dot(high, low_ref[...])


def shift_kernel(grad, shifts):
    tile_rows = shifts.shape[0] * GROUP
    row = lax.broadcasted_iota(jnp.int32, (tile_rows, FREQ), 0)
    lane = lax.broadcasted_iota(jnp.int32, (tile_rows, FREQ), 1)
    lane_bits = lax.broadcasted_iota(jnp.int32, (WINDOW, FREQ), 1)
    below = jnp.zeros((WINDOW - FREQ, FREQ), jnp.float32)
    columns = grad[...].astype(jnp.float32).T.astype(jnp.bfloat16)
    for step in range(tile_rows // GROUP):
        pick = jnp.where(row == GROUP * step + lane // GROUP, 1.0, 0.0).astype(jnp.bfloat16)
        moved = jnp.concatenate([dot(columns, pick), below], axis=0)
        for shift in (8, 4, 2, 1):
            moved = jnp.where(lane_bits & shift != 0, pltpu.roll(moved, shift, 0), moved)
        shifts[step, :HALF] = jnp.zeros((HALF, FREQ), jnp.bfloat16)
        shifts[step, HALF : HALF + WINDOW] = moved.astype(jnp.bfloat16)
        shifts[step, HALF + WINDOW :] = jnp.zeros((HALF - GROUP, FREQ), jnp.bfloat16)


def windows(core, near, far, own, ext, win):
    tile_rows = near.shape[0]
    here = core == 0
    ext[:tile_rows] = jnp.where(here, far[...], near[...])
    ext[tile_rows : 2 * tile_rows] = own[...]
    ext[2 * tile_rows :] = jnp.where(here, near[...], far[...])
    for step in range(tile_rows // GROUP):
        win[:, FREQ * step : FREQ * (step + 1)] = ext[GROUP * step : GROUP * step + WINDOW]


def exchanged(x, lane, width):
    left, right = pltpu.roll(x, HALF - width, 1), pltpu.roll(x, width, 1)
    return jnp.where(lane & width == 0, left, right)


def lags(win, shifts, half, places):
    lane = lax.broadcasted_iota(jnp.int32, (WINDOW - 8, HALF), 1)

    def raw(place):
        first = pl.multiple_of(FREQ - GROUP * place - HALF * half, GROUP)
        taps = shifts[:, pl.ds(first, FREQ), :].reshape(-1, FREQ)
        return dot(win[...], taps)

    def aligned(terms):
        part = terms[: WINDOW - 8, :HALF] + terms[8:, HALF:]
        for shift in (4, 2, 1):
            up = pltpu.roll(part, WINDOW - 8 - shift, 0)
            part = jnp.where(lane & (GROUP * shift) != 0, up, part)
        return part[:FREQ]

    parts, ahead = [], raw(places[0])
    for place in places[1:]:
        terms, ahead = ahead, raw(place)
        parts.append(aligned(terms))
    parts.append(aligned(ahead))
    lane = lax.broadcasted_iota(jnp.int32, (FREQ, HALF), 1)

    def merged(first, second, width):
        low = lane & width == 0
        rest = jnp.where(low, second, first)
        rest = pltpu.roll(rest, width, 1) if width == HALF // 2 else exchanged(rest, lane, width)
        return jnp.where(low, first, second) + rest

    both = merged(merged(parts[0], parts[2], 64), merged(parts[1], parts[3], 64), 32)
    return both + exchanged(both, lane, 16)


def interleaved(even, odd):
    lane = lax.broadcasted_iota(jnp.int32, (FREQ, HALF), 1)
    return jnp.where(lane & GROUP == 0, even, odd)


def by_owner(total):
    flipped = total.T.reshape(HALF // 8, 8, FREQ)
    return jnp.concatenate([flipped[:, :, :HALF], flipped[:, :, HALF:]], axis=1)


def first_kernel(core, far, near, own, shifts, win, even, ext):
    windows(core[0], near, far, own, ext, win)
    even[...] = lags(win, shifts, 1 - core[0], EVEN)


def second_kernel(core, win, shifts, even, out, kept):
    out[...] = by_owner(interleaved(even[...], lags(win, shifts, 1 - core[0], ODD)))
    kept[...] = lags(win, shifts, core[0], EVEN)


def third_kernel(core, win, shifts, kept, keep_z, out):
    out[:, :16] = by_owner(interleaved(kept[...], lags(win, shifts, core[0], ODD)))
    out[:, 16:] = keep_z[...]


def cos_sin(theta):
    turns = jnp.round(theta * (2 / np.pi))
    rest = theta - turns * 1.5703125
    rest = rest - turns * 4.837512969970703e-4
    rest = rest - turns * 7.549789948768648e-8
    square = rest * rest
    sin = rest + rest * square * (
        -1.6666654611e-1 + square * (8.3321608736e-3 + square * -1.9515295891e-4)
    )
    cos = (1.0 - 0.5 * square) + square * square * (
        4.166664568298827e-2 + square * (-1.388731625493765e-3 + square * 2.443315711809948e-5)
    )
    quarter = turns.astype(jnp.int32)
    odd = quarter & 1 != 0
    real, imag = jnp.where(odd, sin, cos), jnp.where(odd, cos, sin)
    real = jnp.where((quarter + 1) & 2 != 0, -real, real)
    imag = jnp.where(quarter & 2 != 0, -imag, imag)
    return real, imag


def field_kernel(
    first, depth, core, defocus, phase, send_k, high, low, keep, send, field_re, field_im, ordered
):
    blocks, rows, width = phase.shape
    for block in range(blocks):
        ordered[depth[0] ^ GATHER_MASKS[block]] = phase[block]
    full = jnp.concatenate([ordered[block] for block in range(blocks)], axis=1)
    centre = (PUPIL - 1) / 2.0
    shape = (rows, PUPIL)
    u = (lax.broadcasted_iota(jnp.int32, shape, 0) + first[0]).astype(jnp.float32)
    v = lax.broadcasted_iota(jnp.int32, shape, 1).astype(jnp.float32)
    radius = (u - centre) ** 2 + (v - centre) ** 2
    limit = (PUPIL / 2.0) ** 2
    inside = radius <= limit
    real, imag = cos_sin(full + defocus[0].astype(jnp.float32) * defocus_step * (radius / limit))
    real, imag = jnp.where(inside, real, 0.0), jnp.where(inside, imag, 0.0)
    field_re[...] = real
    field_im[...] = imag
    terms = dot3(jnp.concatenate([real, imag], axis=0), high, low)
    z_re = terms[:rows, :FREQ] - terms[rows:, FREQ:]
    z_im = terms[:rows, FREQ:] + terms[rows:, :FREQ]
    here = core[0] == 0
    blank = jnp.zeros((rows, FREQ), jnp.float32)
    first_re, second_re = jnp.where(here, z_re, blank), jnp.where(here, blank, z_re)
    first_im, second_im = jnp.where(here, z_im, blank), jnp.where(here, blank, z_im)
    z = jnp.concatenate([first_re, second_re, first_im, second_im], axis=0).T
    z_low, z_high = z[:HALF], z[HALF:]
    keep[...] = jnp.where(here, z_low, z_high).reshape(keep.shape)
    send[:, :16] = send_k[...]
    send[:, 16:] = jnp.where(here, z_high, z_low).reshape(keep.shape)


def middle_kernel(payload, g_high, g_low, s_high, s_low, out):
    chips = payload.shape[0]
    rows = PUPIL // chips
    kernel_grad = payload[0, :16]
    for chip in range(1, chips):
        kernel_grad = kernel_grad + payload[chip, :16]
    kernel_grad = jnp.concatenate([kernel_grad[:8], kernel_grad[8:]], axis=1)
    z_re = jnp.concatenate([payload[chip, 16:, :rows] for chip in range(chips)], axis=1)
    z_im = jnp.concatenate([payload[chip, 16:, rows:] for chip in range(chips)], axis=1)
    terms = dot3(jnp.concatenate([z_re, z_im], axis=0), g_high, g_low)
    y_re = terms[:8, :FREQ] - terms[8:, FREQ:]
    y_im = terms[:8, FREQ:] + terms[8:, :FREQ]
    gy = 2.0 * jnp.concatenate([kernel_grad * y_re, kernel_grad * y_im], axis=0)
    terms = dot3(gy, s_high, s_low)
    gz_re = terms[:8, :PUPIL] + terms[8:, PUPIL:]
    gz_im = terms[8:, :PUPIL] - terms[:8, PUPIL:]
    rows = rows // 2
    for tile in range(2 * chips):
        here = slice(rows * tile, rows * (tile + 1))
        parts = [part[:, here] for part in (gz_re, gz_im)]
        out[tile] = jnp.concatenate([part[half : half + 4] for half in (0, 4) for part in parts], axis=1)


def phase_kernel(payload, field_re, field_im, high, low, out):
    rows = field_re.shape[0]
    gz = payload[...].T
    gz_re = jnp.concatenate([gz[:rows], gz[2 * rows : 3 * rows]], axis=1)
    gz_im = jnp.concatenate([gz[rows : 2 * rows], gz[3 * rows :]], axis=1)
    terms = dot3(jnp.concatenate([gz_re, gz_im], axis=0), high, low)
    ge_re = terms[:rows, :PUPIL] + terms[rows:, PUPIL:]
    ge_im = terms[rows:, :PUPIL] - terms[:rows, PUPIL:]
    phase = field_re[...] * ge_im - field_im[...] * ge_re
    width = out.shape[2]
    for block in range(out.shape[0]):
        out[block] = phase[:, width * block : width * (block + 1)]


def call(kernel, outs, scratch, flops, moved, smem=0):
    def run(*args):
        spaces = [pltpu.SMEM if place < smem else pltpu.VMEM for place in range(len(args))]
        return pl.pallas_call(
            kernel,
            out_shape=outs,
            in_specs=[pl.BlockSpec(memory_space=space) for space in spaces],
            out_specs=jax.tree.map(lambda _: pl.BlockSpec(memory_space=pltpu.VMEM), outs),
            scratch_shapes=scratch,
            compiler_params=pltpu.CompilerParams(vmem_limit_bytes=40 * 2**20),
            cost_estimate=pl.CostEstimate(flops=flops, bytes_accessed=moved, transcendentals=0),
        )(*args)

    return run


def over_depth(x, mask):
    count = lax.axis_size("depth")
    return lax.ppermute(x, "depth", [(i, i ^ mask) for i in range(count)])


def beside(x, tiles):
    pairs = [(i, i + 1) for i in range(1, tiles - 1, 2)]
    return lax.ppermute(x, ("chip", "core"), pairs + [(j, i) for i, j in pairs])


def swap(x):
    return lax.ppermute(x, "core", [(0, 1), (1, 0)])


def body(scene_layers, sensor_grad, pupil_phase, defocus_index):
    chips, depths = lax.axis_size("chip"), lax.axis_size("depth")
    rows, width = pupil_phase.shape
    f32 = jnp.float32
    (g_high, g_low), (s_high, s_low), (r_high, r_low) = freq_tables()
    core, depth, first_row = (
        lax.axis_index(axis).astype(jnp.int32)[None] for axis in ("core", "depth", ("chip", "core"))
    )
    first_row = first_row * rows
    scene = scene_layers[0]
    steps = scene.shape[0] // GROUP
    work = 2 * steps * FREQ * WINDOW * FREQ
    far = beside(scene, 2 * chips)
    other = over_depth(pupil_phase, GATHER_MASKS[1])
    shape, bf16 = jax.ShapeDtypeStruct, jnp.bfloat16
    shifts = call(
        shift_kernel,
        shape((steps, 2 * FREQ, FREQ), bf16),
        [],
        2 * scene.shape[0] * FREQ * FREQ * GROUP,
        2**22,
    )(sensor_grad)
    other, shifts, edge = lax.optimization_barrier((other, shifts, scene))
    near = swap(edge)
    gathered = jnp.stack([pupil_phase, other])
    beyond = over_depth(gathered, GATHER_MASKS[2])
    far, near, shifts = lax.optimization_barrier((far, near, shifts))
    lanes = shape((FREQ, HALF), f32)
    win, even = call(
        first_kernel,
        (shape((WINDOW, steps * FREQ), bf16), lanes),
        [pltpu.VMEM((3 * scene.shape[0], FREQ), bf16)],
        4 * work,
        2**19,
        smem=1,
    )(core, far, near, scene, shifts)
    beyond, win, even = lax.optimization_barrier((beyond, win, even))
    gathered = jnp.concatenate([gathered, beyond], axis=0)
    beyond = over_depth(gathered, GATHER_MASKS[4])
    send_k, even = call(
        second_kernel, (shape((chips, 16, HALF), f32), lanes), [], 8 * work, 2**19, smem=1
    )(core, win, shifts, even)
    beyond, send_k, even = lax.optimization_barrier((beyond, send_k, even))
    gathered = jnp.concatenate([gathered, beyond], axis=0)
    piece, both = shape((chips, 8, HALF), f32), shape((chips, 24, HALF), f32)
    field = shape((rows, PUPIL), f32)
    keep_z, send, field_re, field_im = call(
        field_kernel,
        (piece, both, field, field),
        [pltpu.VMEM((depths, rows, width), f32)],
        2 * 192 * PUPIL * 2 * FREQ,
        3 * 2**20,
        smem=4,
    )(first_row, depth, core, defocus_index, gathered, send_k, g_high, g_low)
    send, win = lax.optimization_barrier((send, win))
    other = swap(send)
    keep = call(third_kernel, both, [], 4 * work, 2**19, smem=1)(core, win, shifts, even, keep_z)
    other, keep = lax.optimization_barrier((other, keep))
    payload = lax.all_to_all(keep + other, "chip", 0, 0, tiled=True)
    payload = call(
        middle_kernel,
        jax.ShapeDtypeStruct((2 * chips, 4, HALF), f32),
        [],
        2 * 96 * PUPIL * 2 * FREQ,
        5 * 2**20,
    )(payload, g_high, g_low, s_high, s_low)
    payload = lax.all_to_all(payload, ("chip", "core"), 0, 0, tiled=True)
    parts = call(
        phase_kernel,
        jax.ShapeDtypeStruct((depths, rows, width), f32),
        [],
        2 * 192 * PUPIL * 2 * FREQ,
        3 * 2**20,
    )(payload.reshape(HALF, HALF), field_re, field_im, r_high, r_low)
    parts = lax.all_to_all(parts, "depth", 0, 0, tiled=True)
    return jnp.sum(parts, axis=0)


def solution(mesh):
    depths, tiles = mesh.devices.shape
    split_mesh = jax.sharding.Mesh(
        mesh.devices.reshape(depths, tiles // 2, 2), ("depth", "chip", "core")
    )
    rows = ("chip", "core")
    placed = (P("depth", rows, None), P(rows, None), P(rows, "depth"), P("depth"))
    return jax.shard_map(
        body, mesh=split_mesh, in_specs=placed, out_specs=P(rows, "depth"), check_vma=False
    )
```

```python
import numpy as np
import jax
import jax.numpy as jnp
import ml_dtypes
from jax import lax
from jax.experimental import pallas as pl
from jax.experimental.pallas import tpu as pltpu
from jax.sharding import PartitionSpec as P

PUPIL = 1024
HALF = 128
FREQ = 2 * HALF
GROUP = 16
GATHER_MASKS = (0, 2, 1, 3, 6, 4, 7, 5)
EVEN, ODD = (0, 2, 4, 6), (1, 3, 5, 7)
WINDOW = FREQ + GROUP
defocus_step = 0.5


def split_table(table):
    high = table.astype(ml_dtypes.bfloat16)
    return high, (table - high.astype(np.float64)).astype(ml_dtypes.bfloat16)


def freq_tables():
    waves = np.arange(FREQ, dtype=np.int64) - HALF
    angle = (waves[:, None] * np.arange(PUPIL)[None, :]) % PUPIL * (2 * np.pi / PUPIL)
    cos, sin = np.cos(angle) * PUPIL**-0.5, -np.sin(angle) * PUPIL**-0.5
    gather = split_table(np.concatenate([cos.T, sin.T], axis=1))
    spread = split_table(np.concatenate([cos, sin], axis=1))
    half, chip, core, row = np.indices((2, FREQ // GROUP, 2, 4)).reshape(4, -1)
    arrived = 128 * (1 - core) + 8 * chip + 4 * half + row
    return gather, spread, [part[arrived] for part in spread]


def split(x):
    high = x.astype(jnp.bfloat16)
    return high, (x - high.astype(jnp.float32)).astype(jnp.bfloat16)


def dot(left, right):
    return jnp.dot(left, right, preferred_element_type=jnp.float32)


def dot3(left, high_ref, low_ref):
    rows = left.shape[0]
    high, low = split(left)
    both = dot(jnp.concatenate([high, low], axis=0), high_ref[...])
    return both[:rows] + both[rows:] + dot(high, low_ref[...])


def shift_kernel(grad, shifts):
    tile_rows = shifts.shape[0] * GROUP
    row = lax.broadcasted_iota(jnp.int32, (tile_rows, FREQ), 0)
    lane = lax.broadcasted_iota(jnp.int32, (tile_rows, FREQ), 1)
    lane_bits = lax.broadcasted_iota(jnp.int32, (WINDOW, FREQ), 1)
    below = jnp.zeros((WINDOW - FREQ, FREQ), jnp.float32)
    columns = grad[...].astype(jnp.float32).T.astype(jnp.bfloat16)
    for step in range(tile_rows // GROUP):
        pick = jnp.where(row == GROUP * step + lane // GROUP, 1.0, 0.0).astype(jnp.bfloat16)
        moved = jnp.concatenate([dot(columns, pick), below], axis=0)
        for shift in (8, 4, 2, 1):
            moved = jnp.where(lane_bits & shift != 0, pltpu.roll(moved, shift, 0), moved)
        shifts[step, :HALF] = jnp.zeros((HALF, FREQ), jnp.bfloat16)
        shifts[step, HALF : HALF + WINDOW] = moved.astype(jnp.bfloat16)
        shifts[step, HALF + WINDOW :] = jnp.zeros((HALF - GROUP, FREQ), jnp.bfloat16)


def windows(core, near, far, own, ext, win):
    tile_rows = near.shape[0]
    here = core == 0
    ext[:tile_rows] = jnp.where(here, far[...], near[...])
    ext[tile_rows : 2 * tile_rows] = own[...]
    ext[2 * tile_rows :] = jnp.where(here, near[...], far[...])
    for step in range(tile_rows // GROUP):
        win[:, FREQ * step : FREQ * (step + 1)] = ext[GROUP * step : GROUP * step + WINDOW]


def exchanged(x, lane, width):
    left, right = pltpu.roll(x, HALF - width, 1), pltpu.roll(x, width, 1)
    return jnp.where(lane & width == 0, left, right)


def lags(win, shifts, half, places):
    lane = lax.broadcasted_iota(jnp.int32, (WINDOW - 8, HALF), 1)

    def raw(place):
        first = pl.multiple_of(FREQ - GROUP * place - HALF * half, GROUP)
        taps = shifts[:, pl.ds(first, FREQ), :].reshape(-1, FREQ)
        return dot(win[...], taps)

    def aligned(terms):
        part = terms[: WINDOW - 8, :HALF] + terms[8:, HALF:]
        for shift in (4, 2, 1):
            up = pltpu.roll(part, WINDOW - 8 - shift, 0)
            part = jnp.where(lane & (GROUP * shift) != 0, up, part)
        return part[:FREQ]

    parts, ahead = [], raw(places[0])
    for place in places[1:]:
        terms, ahead = ahead, raw(place)
        parts.append(aligned(terms))
    parts.append(aligned(ahead))
    lane = lax.broadcasted_iota(jnp.int32, (FREQ, HALF), 1)

    def merged(first, second, width):
        low = lane & width == 0
        rest = jnp.where(low, second, first)
        rest = pltpu.roll(rest, width, 1) if width == HALF // 2 else exchanged(rest, lane, width)
        return jnp.where(low, first, second) + rest

    both = merged(merged(parts[0], parts[2], 64), merged(parts[1], parts[3], 64), 32)
    return both + exchanged(both, lane, 16)


def interleaved(even, odd):
    lane = lax.broadcasted_iota(jnp.int32, (FREQ, HALF), 1)
    return jnp.where(lane & GROUP == 0, even, odd)


def by_owner(total):
    flipped = total.T.reshape(HALF // 8, 8, FREQ)
    return jnp.concatenate([flipped[:, :, :HALF], flipped[:, :, HALF:]], axis=1)


def first_kernel(core, far, near, own, shifts, win, even, ext):
    windows(core[0], near, far, own, ext, win)
    even[...] = lags(win, shifts, 1 - core[0], EVEN)


def second_kernel(core, win, shifts, even, out, kept):
    out[...] = by_owner(interleaved(even[...], lags(win, shifts, 1 - core[0], ODD)))
    kept[...] = lags(win, shifts, core[0], EVEN)


def third_kernel(core, win, shifts, kept, keep_z, out):
    out[:, :16] = by_owner(interleaved(kept[...], lags(win, shifts, core[0], ODD)))
    out[:, 16:] = keep_z[...]


def cos_sin(theta):
    turns = jnp.round(theta * (2 / np.pi))
    rest = theta - turns * 1.5703125
    rest = rest - turns * 4.837512969970703e-4
    rest = rest - turns * 7.549789948768648e-8
    square = rest * rest
    sin = rest + rest * square * (
        -1.6666654611e-1 + square * (8.3321608736e-3 + square * -1.9515295891e-4)
    )
    cos = (1.0 - 0.5 * square) + square * square * (
        4.166664568298827e-2 + square * (-1.388731625493765e-3 + square * 2.443315711809948e-5)
    )
    quarter = turns.astype(jnp.int32)
    odd = quarter & 1 != 0
    real, imag = jnp.where(odd, sin, cos), jnp.where(odd, cos, sin)
    real = jnp.where((quarter + 1) & 2 != 0, -real, real)
    imag = jnp.where(quarter & 2 != 0, -imag, imag)
    return real, imag


def field_kernel(
    first, depth, core, defocus, phase, send_k, high, low, keep, send, field_re, field_im, ordered
):
    blocks, rows, width = phase.shape
    for block in range(blocks):
        ordered[depth[0] ^ GATHER_MASKS[block]] = phase[block]
    full = jnp.concatenate([ordered[block] for block in range(blocks)], axis=1)
    centre = (PUPIL - 1) / 2.0
    shape = (rows, PUPIL)
    u = (lax.broadcasted_iota(jnp.int32, shape, 0) + first[0]).astype(jnp.float32)
    v = lax.broadcasted_iota(jnp.int32, shape, 1).astype(jnp.float32)
    radius = (u - centre) ** 2 + (v - centre) ** 2
    limit = (PUPIL / 2.0) ** 2
    inside = radius <= limit
    real, imag = cos_sin(full + defocus[0].astype(jnp.float32) * defocus_step * (radius / limit))
    real, imag = jnp.where(inside, real, 0.0), jnp.where(inside, imag, 0.0)
    field_re[...] = real
    field_im[...] = imag
    terms = dot3(jnp.concatenate([real, imag], axis=0), high, low)
    z_re = terms[:rows, :FREQ] - terms[rows:, FREQ:]
    z_im = terms[:rows, FREQ:] + terms[rows:, :FREQ]
    here = core[0] == 0
    blank = jnp.zeros((rows, FREQ), jnp.float32)
    first_re, second_re = jnp.where(here, z_re, blank), jnp.where(here, blank, z_re)
    first_im, second_im = jnp.where(here, z_im, blank), jnp.where(here, blank, z_im)
    z = jnp.concatenate([first_re, second_re, first_im, second_im], axis=0).T
    z_low, z_high = z[:HALF], z[HALF:]
    keep[...] = jnp.where(here, z_low, z_high).reshape(keep.shape)
    send[:, :16] = send_k[...]
    send[:, 16:] = jnp.where(here, z_high, z_low).reshape(keep.shape)


def middle_kernel(payload, g_high, g_low, s_high, s_low, out):
    chips = payload.shape[0]
    rows = PUPIL // chips
    kernel_grad = payload[0, :16]
    for chip in range(1, chips):
        kernel_grad = kernel_grad + payload[chip, :16]
    kernel_grad = jnp.concatenate([kernel_grad[:8], kernel_grad[8:]], axis=1)
    order = list(reversed(range(chips)))
    z_re = jnp.concatenate([payload[place, 16:, :rows] for place in order], axis=1)
    z_im = jnp.concatenate([payload[place, 16:, rows:] for place in order], axis=1)
    terms = dot3(jnp.concatenate([z_re, z_im], axis=0), g_high, g_low)
    y_re = terms[:8, :FREQ] - terms[8:, FREQ:]
    y_im = terms[:8, FREQ:] + terms[8:, :FREQ]
    gy = 2.0 * jnp.concatenate([kernel_grad * y_re, kernel_grad * y_im], axis=0)
    terms = dot3(gy, s_high, s_low)
    gz_re = terms[:8, :PUPIL] + terms[8:, PUPIL:]
    gz_im = terms[8:, :PUPIL] - terms[:8, PUPIL:]
    rows = rows // 2
    for tile in range(2 * chips):
        here = slice(rows * tile, rows * (tile + 1))
        parts = [part[:, here] for part in (gz_re, gz_im)]
        rows_of = [part[half : half + 4] for half in (0, 4) for part in parts]
        out[2 * chips - 1 - tile] = jnp.concatenate(rows_of, axis=1)


def phase_kernel(payload, field_re, field_im, high, low, out):
    rows = field_re.shape[0]
    gz = payload[...].T
    gz_re = jnp.concatenate([gz[:rows], gz[2 * rows : 3 * rows]], axis=1)
    gz_im = jnp.concatenate([gz[rows : 2 * rows], gz[3 * rows :]], axis=1)
    terms = dot3(jnp.concatenate([gz_re, gz_im], axis=0), high, low)
    ge_re = terms[:rows, :PUPIL] + terms[rows:, PUPIL:]
    ge_im = terms[rows:, :PUPIL] - terms[:rows, PUPIL:]
    phase = field_re[...] * ge_im - field_im[...] * ge_re
    width = out.shape[2]
    for block in range(out.shape[0]):
        out[out.shape[0] - 1 - block] = phase[:, width * block : width * (block + 1)]


def call(kernel, outs, scratch, flops, moved, smem=0):
    def run(*args):
        spaces = [pltpu.SMEM if place < smem else pltpu.VMEM for place in range(len(args))]
        return pl.pallas_call(
            kernel,
            out_shape=outs,
            in_specs=[pl.BlockSpec(memory_space=space) for space in spaces],
            out_specs=jax.tree.map(lambda _: pl.BlockSpec(memory_space=pltpu.VMEM), outs),
            scratch_shapes=scratch,
            compiler_params=pltpu.CompilerParams(vmem_limit_bytes=40 * 2**20),
            cost_estimate=pl.CostEstimate(flops=flops, bytes_accessed=moved, transcendentals=0),
        )(*args)

    return run


def over_depth(x, mask):
    count = lax.axis_size("depth")
    return lax.ppermute(x, "depth", [(i, i ^ mask) for i in range(count)])


def beside(x, tiles):
    pairs = [(i, i + 1) for i in range(1, tiles - 1, 2)]
    return lax.ppermute(x, ("chip", "core"), pairs + [(j, i) for i, j in pairs])


def redistribute(x, axis):
    order = list(reversed(range(x.shape[0])))
    return lax.all_to_all(x, axis, 0, 0, tiled=True, axis_index_groups=[order])


def swap(x):
    return lax.ppermute(x, "core", [(0, 1), (1, 0)])


def body(scene_layers, sensor_grad, pupil_phase, defocus_index):
    chips, depths = lax.axis_size("chip"), lax.axis_size("depth")
    rows, width = pupil_phase.shape
    f32 = jnp.float32
    (g_high, g_low), (s_high, s_low), (r_high, r_low) = freq_tables()
    core, depth, first_row = (
        lax.axis_index(axis).astype(jnp.int32)[None] for axis in ("core", "depth", ("chip", "core"))
    )
    first_row = first_row * rows
    scene = scene_layers[0]
    steps = scene.shape[0] // GROUP
    work = 2 * steps * FREQ * WINDOW * FREQ
    far = beside(scene, 2 * chips)
    other = over_depth(pupil_phase, GATHER_MASKS[1])
    shape, bf16 = jax.ShapeDtypeStruct, jnp.bfloat16
    shifts = call(
        shift_kernel,
        shape((steps, 2 * FREQ, FREQ), bf16),
        [],
        2 * scene.shape[0] * FREQ * FREQ * GROUP,
        2**22,
    )(sensor_grad)
    other, shifts, edge = lax.optimization_barrier((other, shifts, scene))
    near = swap(edge)
    gathered = jnp.stack([pupil_phase, other])
    beyond = over_depth(gathered, GATHER_MASKS[2])
    far, near, shifts = lax.optimization_barrier((far, near, shifts))
    lanes = shape((FREQ, HALF), f32)
    win, even = call(
        first_kernel,
        (shape((WINDOW, steps * FREQ), bf16), lanes),
        [pltpu.VMEM((3 * scene.shape[0], FREQ), bf16)],
        4 * work,
        2**19,
        smem=1,
    )(core, far, near, scene, shifts)
    beyond, win, even = lax.optimization_barrier((beyond, win, even))
    gathered = jnp.concatenate([gathered, beyond], axis=0)
    beyond = over_depth(gathered, GATHER_MASKS[4])
    send_k, even = call(
        second_kernel, (shape((chips, 16, HALF), f32), lanes), [], 8 * work, 2**19, smem=1
    )(core, win, shifts, even)
    beyond, send_k, even = lax.optimization_barrier((beyond, send_k, even))
    gathered = jnp.concatenate([gathered, beyond], axis=0)
    piece, both = shape((chips, 8, HALF), f32), shape((chips, 24, HALF), f32)
    field = shape((rows, PUPIL), f32)
    keep_z, send, field_re, field_im = call(
        field_kernel,
        (piece, both, field, field),
        [pltpu.VMEM((depths, rows, width), f32)],
        2 * 192 * PUPIL * 2 * FREQ,
        3 * 2**20,
        smem=4,
    )(first_row, depth, core, defocus_index, gathered, send_k, g_high, g_low)
    send, win = lax.optimization_barrier((send, win))
    other = swap(send)
    keep = call(third_kernel, both, [], 4 * work, 2**19, smem=1)(core, win, shifts, even, keep_z)
    other, keep = lax.optimization_barrier((other, keep))
    payload = redistribute(keep + other, "chip")
    payload = call(
        middle_kernel,
        jax.ShapeDtypeStruct((2 * chips, 4, HALF), f32),
        [],
        2 * 96 * PUPIL * 2 * FREQ,
        5 * 2**20,
    )(payload, g_high, g_low, s_high, s_low)
    payload = redistribute(payload, ("chip", "core"))
    parts = call(
        phase_kernel,
        jax.ShapeDtypeStruct((depths, rows, width), f32),
        [],
        2 * 192 * PUPIL * 2 * FREQ,
        3 * 2**20,
    )(payload.reshape(HALF, HALF), field_re, field_im, r_high, r_low)
    parts = redistribute(parts, "depth")
    return jnp.sum(parts, axis=0)


def solution(mesh):
    depths, tiles = mesh.devices.shape
    split_mesh = jax.sharding.Mesh(
        mesh.devices.reshape(depths, tiles // 2, 2), ("depth", "chip", "core")
    )
    rows = ("chip", "core")
    placed = (P("depth", rows, None), P(rows, None), P(rows, "depth"), P("depth"))
    return jax.shard_map(
        body, mesh=split_mesh, in_specs=placed, out_specs=P(rows, "depth"), check_vma=False
    )
```

```python
import numpy as np
import jax
import jax.numpy as jnp
import ml_dtypes
from jax import lax
from jax.experimental import pallas as pl
from jax.experimental.pallas import tpu as pltpu
from jax.sharding import PartitionSpec as P

PUPIL = 1024
HALF = 128
FREQ = 2 * HALF
GROUP = 16
GATHER_MASKS = (0, 2, 1, 3, 6, 4, 7, 5)
CHIP_ORDER = tuple(8 * y + z for z in reversed(range(8)) for y in (1, 0))
TILE_ORDER = tuple(2 * chip + core for chip in CHIP_ORDER for core in (1, 0))
DEPTH_ORDER = tuple(reversed(range(8)))
EVEN, ODD = (0, 2, 4, 6), (1, 3, 5, 7)
WINDOW = FREQ + GROUP
defocus_step = 0.5


def split_table(table):
    high = table.astype(ml_dtypes.bfloat16)
    return high, (table - high.astype(np.float64)).astype(ml_dtypes.bfloat16)


def freq_tables():
    waves = np.arange(FREQ, dtype=np.int64) - HALF
    angle = (waves[:, None] * np.arange(PUPIL)[None, :]) % PUPIL * (2 * np.pi / PUPIL)
    cos, sin = np.cos(angle) * PUPIL**-0.5, -np.sin(angle) * PUPIL**-0.5
    gather = split_table(np.concatenate([cos.T, sin.T], axis=1))
    spread = split_table(np.concatenate([cos, sin], axis=1))
    half, place, row = np.indices((2, len(TILE_ORDER), 4)).reshape(3, -1)
    tile = np.array(TILE_ORDER)[place]
    arrived = 128 * (tile % 2) + 8 * np.argsort(CHIP_ORDER)[tile // 2] + 4 * half + row
    return gather, spread, [part[arrived] for part in spread]


def split(x):
    high = x.astype(jnp.bfloat16)
    return high, (x - high.astype(jnp.float32)).astype(jnp.bfloat16)


def dot(left, right):
    return jnp.dot(left, right, preferred_element_type=jnp.float32)


def dot3(left, high_ref, low_ref):
    rows = left.shape[0]
    high, low = split(left)
    both = dot(jnp.concatenate([high, low], axis=0), high_ref[...])
    return both[:rows] + both[rows:] + dot(high, low_ref[...])


def shift_kernel(grad, shifts):
    tile_rows = shifts.shape[0] * GROUP
    row = lax.broadcasted_iota(jnp.int32, (tile_rows, FREQ), 0)
    lane = lax.broadcasted_iota(jnp.int32, (tile_rows, FREQ), 1)
    lane_bits = lax.broadcasted_iota(jnp.int32, (WINDOW, FREQ), 1)
    below = jnp.zeros((WINDOW - FREQ, FREQ), jnp.float32)
    columns = grad[...].astype(jnp.float32).T.astype(jnp.bfloat16)
    for step in range(tile_rows // GROUP):
        pick = jnp.where(row == GROUP * step + lane // GROUP, 1.0, 0.0).astype(jnp.bfloat16)
        moved = jnp.concatenate([dot(columns, pick), below], axis=0)
        for shift in (8, 4, 2, 1):
            moved = jnp.where(lane_bits & shift != 0, pltpu.roll(moved, shift, 0), moved)
        shifts[step, :HALF] = jnp.zeros((HALF, FREQ), jnp.bfloat16)
        shifts[step, HALF : HALF + WINDOW] = moved.astype(jnp.bfloat16)
        shifts[step, HALF + WINDOW :] = jnp.zeros((HALF - GROUP, FREQ), jnp.bfloat16)


def windows(core, near, far, own, ext, win):
    tile_rows = near.shape[0]
    here = core == 0
    ext[:tile_rows] = jnp.where(here, far[...], near[...])
    ext[tile_rows : 2 * tile_rows] = own[...]
    ext[2 * tile_rows :] = jnp.where(here, near[...], far[...])
    for step in range(tile_rows // GROUP):
        win[:, FREQ * step : FREQ * (step + 1)] = ext[GROUP * step : GROUP * step + WINDOW]


def exchanged(x, lane, width):
    left, right = pltpu.roll(x, HALF - width, 1), pltpu.roll(x, width, 1)
    return jnp.where(lane & width == 0, left, right)


def lags(win, shifts, half, places):
    lane = lax.broadcasted_iota(jnp.int32, (WINDOW - 8, HALF), 1)

    def raw(place):
        first = pl.multiple_of(FREQ - GROUP * place - HALF * half, GROUP)
        taps = shifts[:, pl.ds(first, FREQ), :].reshape(-1, FREQ)
        return dot(win[...], taps)

    def aligned(terms):
        part = terms[: WINDOW - 8, :HALF] + terms[8:, HALF:]
        for shift in (4, 2, 1):
            up = pltpu.roll(part, WINDOW - 8 - shift, 0)
            part = jnp.where(lane & (GROUP * shift) != 0, up, part)
        return part[:FREQ]

    parts, ahead = [], raw(places[0])
    for place in places[1:]:
        terms, ahead = ahead, raw(place)
        parts.append(aligned(terms))
    parts.append(aligned(ahead))
    lane = lax.broadcasted_iota(jnp.int32, (FREQ, HALF), 1)

    def merged(first, second, width):
        low = lane & width == 0
        rest = jnp.where(low, second, first)
        rest = pltpu.roll(rest, width, 1) if width == HALF // 2 else exchanged(rest, lane, width)
        return jnp.where(low, first, second) + rest

    both = merged(merged(parts[0], parts[2], 64), merged(parts[1], parts[3], 64), 32)
    return both + exchanged(both, lane, 16)


def interleaved(even, odd):
    lane = lax.broadcasted_iota(jnp.int32, (FREQ, HALF), 1)
    return jnp.where(lane & GROUP == 0, even, odd)


def by_owner(total):
    flipped = total.T.reshape(HALF // 8, 8, FREQ)
    return jnp.concatenate([flipped[:, :, :HALF], flipped[:, :, HALF:]], axis=1)


def first_kernel(core, far, near, own, shifts, win, even, ext):
    windows(core[0], near, far, own, ext, win)
    even[...] = lags(win, shifts, 1 - core[0], EVEN)


def second_kernel(core, win, shifts, even, out, kept):
    out[...] = by_owner(interleaved(even[...], lags(win, shifts, 1 - core[0], ODD)))
    kept[...] = lags(win, shifts, core[0], EVEN)


def third_kernel(core, win, shifts, kept, keep_z, out):
    out[:, :16] = by_owner(interleaved(kept[...], lags(win, shifts, core[0], ODD)))
    out[:, 16:] = keep_z[...]


def cos_sin(theta):
    turns = jnp.round(theta * (2 / np.pi))
    rest = theta - turns * 1.5703125
    rest = rest - turns * 4.837512969970703e-4
    rest = rest - turns * 7.549789948768648e-8
    square = rest * rest
    sin = rest + rest * square * (
        -1.6666654611e-1 + square * (8.3321608736e-3 + square * -1.9515295891e-4)
    )
    cos = (1.0 - 0.5 * square) + square * square * (
        4.166664568298827e-2 + square * (-1.388731625493765e-3 + square * 2.443315711809948e-5)
    )
    quarter = turns.astype(jnp.int32)
    odd = quarter & 1 != 0
    real, imag = jnp.where(odd, sin, cos), jnp.where(odd, cos, sin)
    real = jnp.where((quarter + 1) & 2 != 0, -real, real)
    imag = jnp.where(quarter & 2 != 0, -imag, imag)
    return real, imag


def field_kernel(
    first, depth, core, defocus, phase, send_k, high, low, keep, send, field_re, field_im, ordered
):
    blocks, rows, width = phase.shape
    for block in range(blocks):
        ordered[depth[0] ^ GATHER_MASKS[block]] = phase[block]
    full = jnp.concatenate([ordered[block] for block in range(blocks)], axis=1)
    centre = (PUPIL - 1) / 2.0
    shape = (rows, PUPIL)
    u = (lax.broadcasted_iota(jnp.int32, shape, 0) + first[0]).astype(jnp.float32)
    v = lax.broadcasted_iota(jnp.int32, shape, 1).astype(jnp.float32)
    radius = (u - centre) ** 2 + (v - centre) ** 2
    limit = (PUPIL / 2.0) ** 2
    inside = radius <= limit
    real, imag = cos_sin(full + defocus[0].astype(jnp.float32) * defocus_step * (radius / limit))
    real, imag = jnp.where(inside, real, 0.0), jnp.where(inside, imag, 0.0)
    field_re[...] = real
    field_im[...] = imag
    terms = dot3(jnp.concatenate([real, imag], axis=0), high, low)
    z_re = terms[:rows, :FREQ] - terms[rows:, FREQ:]
    z_im = terms[:rows, FREQ:] + terms[rows:, :FREQ]
    here = core[0] == 0
    blank = jnp.zeros((rows, FREQ), jnp.float32)
    first_re, second_re = jnp.where(here, z_re, blank), jnp.where(here, blank, z_re)
    first_im, second_im = jnp.where(here, z_im, blank), jnp.where(here, blank, z_im)
    z = jnp.concatenate([first_re, second_re, first_im, second_im], axis=0).T
    z_low, z_high = z[:HALF], z[HALF:]
    keep[...] = jnp.where(here, z_low, z_high).reshape(keep.shape)
    send[:, :16] = send_k[...]
    send[:, 16:] = jnp.where(here, z_high, z_low).reshape(keep.shape)


def middle_kernel(payload, g_high, g_low, s_high, s_low, out):
    chips = payload.shape[0]
    rows = PUPIL // chips
    kernel_grad = payload[0, :16]
    for chip in range(1, chips):
        kernel_grad = kernel_grad + payload[chip, :16]
    kernel_grad = jnp.concatenate([kernel_grad[:8], kernel_grad[8:]], axis=1)
    order = [CHIP_ORDER.index(chip) for chip in range(chips)]
    z_re = jnp.concatenate([payload[place, 16:, :rows] for place in order], axis=1)
    z_im = jnp.concatenate([payload[place, 16:, rows:] for place in order], axis=1)
    terms = dot3(jnp.concatenate([z_re, z_im], axis=0), g_high, g_low)
    y_re = terms[:8, :FREQ] - terms[8:, FREQ:]
    y_im = terms[:8, FREQ:] + terms[8:, :FREQ]
    gy = 2.0 * jnp.concatenate([kernel_grad * y_re, kernel_grad * y_im], axis=0)
    terms = dot3(gy, s_high, s_low)
    gz_re = terms[:8, :PUPIL] + terms[8:, PUPIL:]
    gz_im = terms[8:, :PUPIL] - terms[:8, PUPIL:]
    rows = rows // 2
    for tile in range(2 * chips):
        here = slice(rows * tile, rows * (tile + 1))
        parts = [part[:, here] for part in (gz_re, gz_im)]
        rows_of = [part[half : half + 4] for half in (0, 4) for part in parts]
        out[TILE_ORDER.index(tile)] = jnp.concatenate(rows_of, axis=1)


def phase_kernel(payload, field_re, field_im, high, low, out):
    rows = field_re.shape[0]
    gz = payload[...].T
    gz_re = jnp.concatenate([gz[:rows], gz[2 * rows : 3 * rows]], axis=1)
    gz_im = jnp.concatenate([gz[rows : 2 * rows], gz[3 * rows :]], axis=1)
    terms = dot3(jnp.concatenate([gz_re, gz_im], axis=0), high, low)
    ge_re = terms[:rows, :PUPIL] + terms[rows:, PUPIL:]
    ge_im = terms[rows:, :PUPIL] - terms[:rows, PUPIL:]
    phase = field_re[...] * ge_im - field_im[...] * ge_re
    width = out.shape[2]
    for block in range(out.shape[0]):
        out[DEPTH_ORDER.index(block)] = phase[:, width * block : width * (block + 1)]


def call(kernel, outs, scratch, flops, moved, smem=0):
    def run(*args):
        spaces = [pltpu.SMEM if place < smem else pltpu.VMEM for place in range(len(args))]
        return pl.pallas_call(
            kernel,
            out_shape=outs,
            in_specs=[pl.BlockSpec(memory_space=space) for space in spaces],
            out_specs=jax.tree.map(lambda _: pl.BlockSpec(memory_space=pltpu.VMEM), outs),
            scratch_shapes=scratch,
            compiler_params=pltpu.CompilerParams(vmem_limit_bytes=40 * 2**20),
            cost_estimate=pl.CostEstimate(flops=flops, bytes_accessed=moved, transcendentals=0),
        )(*args)

    return run


def over_depth(x, mask):
    count = lax.axis_size("depth")
    return lax.ppermute(x, "depth", [(i, i ^ mask) for i in range(count)])


def beside(x, tiles):
    pairs = [(i, i + 1) for i in range(1, tiles - 1, 2)]
    return lax.ppermute(x, ("chip", "core"), pairs + [(j, i) for i, j in pairs])


def redistribute(x, axis, order):
    return lax.all_to_all(x, axis, 0, 0, tiled=True, axis_index_groups=[list(order)])


def swap(x):
    return lax.ppermute(x, "core", [(0, 1), (1, 0)])


def body(scene_layers, sensor_grad, pupil_phase, defocus_index):
    chips, depths = lax.axis_size("chip"), lax.axis_size("depth")
    rows, width = pupil_phase.shape
    f32 = jnp.float32
    (g_high, g_low), (s_high, s_low), (r_high, r_low) = freq_tables()
    core, depth, first_row = (
        lax.axis_index(axis).astype(jnp.int32)[None] for axis in ("core", "depth", ("chip", "core"))
    )
    first_row = first_row * rows
    scene = scene_layers[0]
    steps = scene.shape[0] // GROUP
    work = 2 * steps * FREQ * WINDOW * FREQ
    far = beside(scene, 2 * chips)
    other = over_depth(pupil_phase, GATHER_MASKS[1])
    shape, bf16 = jax.ShapeDtypeStruct, jnp.bfloat16
    shifts = call(
        shift_kernel,
        shape((steps, 2 * FREQ, FREQ), bf16),
        [],
        2 * scene.shape[0] * FREQ * FREQ * GROUP,
        2**22,
    )(sensor_grad)
    other, shifts, edge = lax.optimization_barrier((other, shifts, scene))
    near = swap(edge)
    gathered = jnp.stack([pupil_phase, other])
    beyond = over_depth(gathered, GATHER_MASKS[2])
    far, near, shifts = lax.optimization_barrier((far, near, shifts))
    lanes = shape((FREQ, HALF), f32)
    win, even = call(
        first_kernel,
        (shape((WINDOW, steps * FREQ), bf16), lanes),
        [pltpu.VMEM((3 * scene.shape[0], FREQ), bf16)],
        4 * work,
        2**19,
        smem=1,
    )(core, far, near, scene, shifts)
    beyond, win, even = lax.optimization_barrier((beyond, win, even))
    gathered = jnp.concatenate([gathered, beyond], axis=0)
    beyond = over_depth(gathered, GATHER_MASKS[4])
    send_k, even = call(
        second_kernel, (shape((chips, 16, HALF), f32), lanes), [], 8 * work, 2**19, smem=1
    )(core, win, shifts, even)
    beyond, send_k, even = lax.optimization_barrier((beyond, send_k, even))
    gathered = jnp.concatenate([gathered, beyond], axis=0)
    piece, both = shape((chips, 8, HALF), f32), shape((chips, 24, HALF), f32)
    field = shape((rows, PUPIL), f32)
    keep_z, send, field_re, field_im = call(
        field_kernel,
        (piece, both, field, field),
        [pltpu.VMEM((depths, rows, width), f32)],
        2 * 192 * PUPIL * 2 * FREQ,
        3 * 2**20,
        smem=4,
    )(first_row, depth, core, defocus_index, gathered, send_k, g_high, g_low)
    send, win = lax.optimization_barrier((send, win))
    other = swap(send)
    keep = call(third_kernel, both, [], 4 * work, 2**19, smem=1)(core, win, shifts, even, keep_z)
    other, keep = lax.optimization_barrier((other, keep))
    payload = redistribute(keep + other, "chip", CHIP_ORDER)
    payload = call(
        middle_kernel,
        jax.ShapeDtypeStruct((2 * chips, 4, HALF), f32),
        [],
        2 * 96 * PUPIL * 2 * FREQ,
        5 * 2**20,
    )(payload, g_high, g_low, s_high, s_low)
    payload = redistribute(payload, ("chip", "core"), TILE_ORDER)
    parts = call(
        phase_kernel,
        jax.ShapeDtypeStruct((depths, rows, width), f32),
        [],
        2 * 192 * PUPIL * 2 * FREQ,
        3 * 2**20,
    )(payload.reshape(HALF, HALF), field_re, field_im, r_high, r_low)
    parts = redistribute(parts, "depth", DEPTH_ORDER)
    return jnp.sum(parts, axis=0)


def solution(mesh):
    depths, tiles = mesh.devices.shape
    split_mesh = jax.sharding.Mesh(
        mesh.devices.reshape(depths, tiles // 2, 2), ("depth", "chip", "core")
    )
    rows = ("chip", "core")
    placed = (P("depth", rows, None), P(rows, None), P(rows, "depth"), P("depth"))
    return jax.shard_map(
        body, mesh=split_mesh, in_specs=placed, out_specs=P(rows, "depth"), check_vma=False
    )
```

```python
import numpy as np
import jax
import jax.numpy as jnp
import ml_dtypes
from jax import lax
from jax.experimental import pallas as pl
from jax.experimental.pallas import tpu as pltpu
from jax.sharding import PartitionSpec as P

PUPIL = 1024
HALF = 128
FREQ = 2 * HALF
GROUP = 16
GATHER_MASKS = (0, 2, 1, 3, 6, 4, 7, 5)
CHIPS = tuple(8 * y + z for z in reversed(range(8)) for y in (1, 0))
CHIP_ORDERS = (CHIPS, CHIPS[8:] + CHIPS[:8])
TILE_ORDER = tuple(
    16 * y + 2 * z + core
    for _, z, y, core in sorted(
        ((z + 1.5 * (y ^ core), z, y, core) for z in range(8) for y in (0, 1) for core in (0, 1)),
        reverse=True,
    )
)
EVEN, ODD = (0, 2, 4, 6), (1, 3, 5, 7)
WINDOW = FREQ + GROUP
defocus_step = 0.5


def split_table(table):
    high = table.astype(ml_dtypes.bfloat16)
    return high, (table - high.astype(np.float64)).astype(ml_dtypes.bfloat16)


def freq_tables():
    waves = np.arange(FREQ, dtype=np.int64) - HALF
    angle = (waves[:, None] * np.arange(PUPIL)[None, :]) % PUPIL * (2 * np.pi / PUPIL)
    cos, sin = np.cos(angle) * PUPIL**-0.5, -np.sin(angle) * PUPIL**-0.5
    gather = split_table(np.concatenate([cos.T, sin.T], axis=1))
    spread = split_table(np.concatenate([cos, sin], axis=1))
    half, place, row = np.indices((2, len(TILE_ORDER), 4)).reshape(3, -1)
    tile = np.array(TILE_ORDER)[place]
    owned = np.argsort(CHIP_ORDERS, axis=1)[tile % 2, tile // 2]
    arrived = 128 * (tile % 2) + 8 * owned + 4 * half + row
    return gather, spread, [part[arrived] for part in spread]


def split(x):
    high = x.astype(jnp.bfloat16)
    return high, (x - high.astype(jnp.float32)).astype(jnp.bfloat16)


def dot(left, right):
    return jnp.dot(left, right, preferred_element_type=jnp.float32)


def dot3(left, high_ref, low_ref):
    rows = left.shape[0]
    high, low = split(left)
    both = dot(jnp.concatenate([high, low], axis=0), high_ref[...])
    return both[:rows] + both[rows:] + dot(high, low_ref[...])


def shift_kernel(grad, shifts):
    tile_rows = shifts.shape[0] * GROUP
    row = lax.broadcasted_iota(jnp.int32, (tile_rows, FREQ), 0)
    lane = lax.broadcasted_iota(jnp.int32, (tile_rows, FREQ), 1)
    lane_bits = lax.broadcasted_iota(jnp.int32, (WINDOW, FREQ), 1)
    below = jnp.zeros((WINDOW - FREQ, FREQ), jnp.float32)
    columns = grad[...].astype(jnp.float32).T.astype(jnp.bfloat16)
    for step in range(tile_rows // GROUP):
        pick = jnp.where(row == GROUP * step + lane // GROUP, 1.0, 0.0).astype(jnp.bfloat16)
        moved = jnp.concatenate([dot(columns, pick), below], axis=0)
        for shift in (8, 4, 2, 1):
            moved = jnp.where(lane_bits & shift != 0, pltpu.roll(moved, shift, 0), moved)
        shifts[step, :HALF] = jnp.zeros((HALF, FREQ), jnp.bfloat16)
        shifts[step, HALF : HALF + WINDOW] = moved.astype(jnp.bfloat16)
        shifts[step, HALF + WINDOW :] = jnp.zeros((HALF - GROUP, FREQ), jnp.bfloat16)


def windows(core, near, far, own, ext, win):
    tile_rows = near.shape[0]
    here = core == 0
    ext[:tile_rows] = jnp.where(here, far[...], near[...])
    ext[tile_rows : 2 * tile_rows] = own[...]
    ext[2 * tile_rows :] = jnp.where(here, near[...], far[...])
    for step in range(tile_rows // GROUP):
        win[:, FREQ * step : FREQ * (step + 1)] = ext[GROUP * step : GROUP * step + WINDOW]


def exchanged(x, lane, width):
    left, right = pltpu.roll(x, HALF - width, 1), pltpu.roll(x, width, 1)
    return jnp.where(lane & width == 0, left, right)


def lags(win, shifts, half, places):
    lane = lax.broadcasted_iota(jnp.int32, (WINDOW - 8, HALF), 1)

    def raw(place):
        first = pl.multiple_of(FREQ - GROUP * place - HALF * half, GROUP)
        taps = shifts[:, pl.ds(first, FREQ), :].reshape(-1, FREQ)
        return dot(win[...], taps)

    def aligned(terms):
        part = terms[: WINDOW - 8, :HALF] + terms[8:, HALF:]
        for shift in (4, 2, 1):
            up = pltpu.roll(part, WINDOW - 8 - shift, 0)
            part = jnp.where(lane & (GROUP * shift) != 0, up, part)
        return part[:FREQ]

    parts, ahead = [], raw(places[0])
    for place in places[1:]:
        terms, ahead = ahead, raw(place)
        parts.append(aligned(terms))
    parts.append(aligned(ahead))
    lane = lax.broadcasted_iota(jnp.int32, (FREQ, HALF), 1)

    def merged(first, second, width):
        low = lane & width == 0
        rest = jnp.where(low, second, first)
        rest = pltpu.roll(rest, width, 1) if width == HALF // 2 else exchanged(rest, lane, width)
        return jnp.where(low, first, second) + rest

    both = merged(merged(parts[0], parts[2], 64), merged(parts[1], parts[3], 64), 32)
    return both + exchanged(both, lane, 16)


def interleaved(even, odd):
    lane = lax.broadcasted_iota(jnp.int32, (FREQ, HALF), 1)
    return jnp.where(lane & GROUP == 0, even, odd)


def by_owner(total):
    flipped = total.T.reshape(HALF // 8, 8, FREQ)
    return jnp.concatenate([flipped[:, :, :HALF], flipped[:, :, HALF:]], axis=1)


def first_kernel(core, far, near, own, shifts, win, even, ext):
    windows(core[0], near, far, own, ext, win)
    even[...] = lags(win, shifts, 1 - core[0], EVEN)


def second_kernel(core, win, shifts, even, out, kept):
    out[...] = by_owner(interleaved(even[...], lags(win, shifts, 1 - core[0], ODD)))
    kept[...] = lags(win, shifts, core[0], EVEN)


def third_kernel(core, win, shifts, kept, keep_z, out):
    out[:, :16] = by_owner(interleaved(kept[...], lags(win, shifts, core[0], ODD)))
    out[:, 16:] = keep_z[...]


def cos_sin(theta):
    turns = jnp.round(theta * (2 / np.pi))
    rest = theta - turns * 1.5703125
    rest = rest - turns * 4.837512969970703e-4
    rest = rest - turns * 7.549789948768648e-8
    square = rest * rest
    sin = rest + rest * square * (
        -1.6666654611e-1 + square * (8.3321608736e-3 + square * -1.9515295891e-4)
    )
    cos = (1.0 - 0.5 * square) + square * square * (
        4.166664568298827e-2 + square * (-1.388731625493765e-3 + square * 2.443315711809948e-5)
    )
    quarter = turns.astype(jnp.int32)
    odd = quarter & 1 != 0
    real, imag = jnp.where(odd, sin, cos), jnp.where(odd, cos, sin)
    real = jnp.where((quarter + 1) & 2 != 0, -real, real)
    imag = jnp.where(quarter & 2 != 0, -imag, imag)
    return real, imag


def field_kernel(
    first, depth, core, defocus, phase, send_k, high, low, keep, send, field_re, field_im, ordered
):
    blocks, rows, width = phase.shape
    for block in range(blocks):
        ordered[depth[0] ^ GATHER_MASKS[block]] = phase[block]
    full = jnp.concatenate([ordered[block] for block in range(blocks)], axis=1)
    centre = (PUPIL - 1) / 2.0
    shape = (rows, PUPIL)
    u = (lax.broadcasted_iota(jnp.int32, shape, 0) + first[0]).astype(jnp.float32)
    v = lax.broadcasted_iota(jnp.int32, shape, 1).astype(jnp.float32)
    radius = (u - centre) ** 2 + (v - centre) ** 2
    limit = (PUPIL / 2.0) ** 2
    inside = radius <= limit
    real, imag = cos_sin(full + defocus[0].astype(jnp.float32) * defocus_step * (radius / limit))
    real, imag = jnp.where(inside, real, 0.0), jnp.where(inside, imag, 0.0)
    field_re[...] = real
    field_im[...] = imag
    terms = dot3(jnp.concatenate([real, imag], axis=0), high, low)
    z_re = terms[:rows, :FREQ] - terms[rows:, FREQ:]
    z_im = terms[:rows, FREQ:] + terms[rows:, :FREQ]
    here = core[0] == 0
    blank = jnp.zeros((rows, FREQ), jnp.float32)
    first_re, second_re = jnp.where(here, z_re, blank), jnp.where(here, blank, z_re)
    first_im, second_im = jnp.where(here, z_im, blank), jnp.where(here, blank, z_im)
    z = jnp.concatenate([first_re, second_re, first_im, second_im], axis=0).T
    z_low, z_high = z[:HALF], z[HALF:]
    keep[...] = jnp.where(here, z_low, z_high).reshape(keep.shape)
    send[:, :16] = send_k[...]
    send[:, 16:] = jnp.where(here, z_high, z_low).reshape(keep.shape)


def middle_kernel(core, payload, g_high, g_low, s_high, s_low, out):
    chips = payload.shape[0]
    rows = PUPIL // chips
    kernel_grad = payload[0, :16]
    for chip in range(1, chips):
        kernel_grad = kernel_grad + payload[chip, :16]
    kernel_grad = jnp.concatenate([kernel_grad[:8], kernel_grad[8:]], axis=1)
    blocks = [[payload[order.index(chip), 16:] for order in CHIP_ORDERS] for chip in range(chips)]
    blocks = [jnp.where(core[0] == 0, *pair) for pair in blocks]
    z_re = jnp.concatenate([block[:, :rows] for block in blocks], axis=1)
    z_im = jnp.concatenate([block[:, rows:] for block in blocks], axis=1)
    terms = dot3(jnp.concatenate([z_re, z_im], axis=0), g_high, g_low)
    y_re = terms[:8, :FREQ] - terms[8:, FREQ:]
    y_im = terms[:8, FREQ:] + terms[8:, :FREQ]
    gy = 2.0 * jnp.concatenate([kernel_grad * y_re, kernel_grad * y_im], axis=0)
    terms = dot3(gy, s_high, s_low)
    gz_re = terms[:8, :PUPIL] + terms[8:, PUPIL:]
    gz_im = terms[8:, :PUPIL] - terms[:8, PUPIL:]
    rows = rows // 2
    for tile in range(2 * chips):
        here = slice(rows * tile, rows * (tile + 1))
        parts = [part[:, here] for part in (gz_re, gz_im)]
        rows_of = [part[half : half + 4] for half in (0, 4) for part in parts]
        out[TILE_ORDER.index(tile)] = jnp.concatenate(rows_of, axis=1)


def phase_kernel(core, payload, field_re, field_im, high, low, out):
    rows = field_re.shape[0]
    gz = payload[...].T
    gz_re = jnp.concatenate([gz[:rows], gz[2 * rows : 3 * rows]], axis=1)
    gz_im = jnp.concatenate([gz[rows : 2 * rows], gz[3 * rows :]], axis=1)
    terms = dot3(jnp.concatenate([gz_re, gz_im], axis=0), high, low)
    ge_re = terms[:rows, :PUPIL] + terms[rows:, PUPIL:]
    ge_im = terms[rows:, :PUPIL] - terms[:rows, PUPIL:]
    phase = field_re[...] * ge_im - field_im[...] * ge_re
    width = out.shape[2]
    for block in range(out.shape[0]):
        place = (out.shape[0] - 1 - block + 4 * core[0]) & (out.shape[0] - 1)
        out[place] = phase[:, width * block : width * (block + 1)]


def call(kernel, outs, scratch, flops, moved, smem=0):
    def run(*args):
        spaces = [pltpu.SMEM if place < smem else pltpu.VMEM for place in range(len(args))]
        return pl.pallas_call(
            kernel,
            out_shape=outs,
            in_specs=[pl.BlockSpec(memory_space=space) for space in spaces],
            out_specs=jax.tree.map(lambda _: pl.BlockSpec(memory_space=pltpu.VMEM), outs),
            scratch_shapes=scratch,
            compiler_params=pltpu.CompilerParams(vmem_limit_bytes=40 * 2**20),
            cost_estimate=pl.CostEstimate(flops=flops, bytes_accessed=moved, transcendentals=0),
        )(*args)

    return run


def over_depth(x, mask):
    count = lax.axis_size("depth")
    return lax.ppermute(x, "depth", [(i, i ^ mask) for i in range(count)])


def beside(x, tiles):
    pairs = [(i, i + 1) for i in range(1, tiles - 1, 2)]
    return lax.ppermute(x, ("chip", "core"), pairs + [(j, i) for i, j in pairs])


def redistribute(x, axis, groups):
    return lax.all_to_all(x, axis, 0, 0, tiled=True, axis_index_groups=groups)


def swap(x):
    return lax.ppermute(x, "core", [(0, 1), (1, 0)])


def body(scene_layers, sensor_grad, pupil_phase, defocus_index):
    chips, depths = lax.axis_size("chip"), lax.axis_size("depth")
    rows, width = pupil_phase.shape
    f32 = jnp.float32
    (g_high, g_low), (s_high, s_low), (r_high, r_low) = freq_tables()
    core, depth, first_row = (
        lax.axis_index(axis).astype(jnp.int32)[None] for axis in ("core", "depth", ("chip", "core"))
    )
    first_row = first_row * rows
    scene = scene_layers[0]
    steps = scene.shape[0] // GROUP
    work = 2 * steps * FREQ * WINDOW * FREQ
    far = beside(scene, 2 * chips)
    other = over_depth(pupil_phase, GATHER_MASKS[1])
    shape, bf16 = jax.ShapeDtypeStruct, jnp.bfloat16
    shifts = call(
        shift_kernel,
        shape((steps, 2 * FREQ, FREQ), bf16),
        [],
        2 * scene.shape[0] * FREQ * FREQ * GROUP,
        2**22,
    )(sensor_grad)
    other, shifts, edge = lax.optimization_barrier((other, shifts, scene))
    near = swap(edge)
    gathered = jnp.stack([pupil_phase, other])
    beyond = over_depth(gathered, GATHER_MASKS[2])
    far, near, shifts = lax.optimization_barrier((far, near, shifts))
    lanes = shape((FREQ, HALF), f32)
    win, even = call(
        first_kernel,
        (shape((WINDOW, steps * FREQ), bf16), lanes),
        [pltpu.VMEM((3 * scene.shape[0], FREQ), bf16)],
        4 * work,
        2**19,
        smem=1,
    )(core, far, near, scene, shifts)
    beyond, win, even = lax.optimization_barrier((beyond, win, even))
    gathered = jnp.concatenate([gathered, beyond], axis=0)
    beyond = over_depth(gathered, GATHER_MASKS[4])
    send_k, even = call(
        second_kernel, (shape((chips, 16, HALF), f32), lanes), [], 8 * work, 2**19, smem=1
    )(core, win, shifts, even)
    beyond, send_k, even = lax.optimization_barrier((beyond, send_k, even))
    gathered = jnp.concatenate([gathered, beyond], axis=0)
    piece, both = shape((chips, 8, HALF), f32), shape((chips, 24, HALF), f32)
    field = shape((rows, PUPIL), f32)
    keep_z, send, field_re, field_im = call(
        field_kernel,
        (piece, both, field, field),
        [pltpu.VMEM((depths, rows, width), f32)],
        2 * 192 * PUPIL * 2 * FREQ,
        3 * 2**20,
        smem=4,
    )(first_row, depth, core, defocus_index, gathered, send_k, g_high, g_low)
    send, win = lax.optimization_barrier((send, win))
    other = swap(send)
    keep = call(third_kernel, both, [], 4 * work, 2**19, smem=1)(core, win, shifts, even, keep_z)
    other, keep = lax.optimization_barrier((other, keep))
    groups = [[2 * chip + place for chip in CHIP_ORDERS[place]] for place in range(2)]
    payload = redistribute(keep + other, ("chip", "core"), groups)
    payload = call(
        middle_kernel,
        jax.ShapeDtypeStruct((2 * chips, 4, HALF), f32),
        [],
        2 * 96 * PUPIL * 2 * FREQ,
        5 * 2**20,
        smem=1,
    )(core, payload, g_high, g_low, s_high, s_low)
    payload = redistribute(payload, ("chip", "core"), [list(TILE_ORDER)])
    parts = call(
        phase_kernel,
        jax.ShapeDtypeStruct((depths, rows, width), f32),
        [],
        2 * 192 * PUPIL * 2 * FREQ,
        3 * 2**20,
        smem=1,
    )(core, payload.reshape(HALF, HALF), field_re, field_im, r_high, r_low)
    groups = [
        [(depths - 1 - place + 4 * tile) % depths * 2 * chips + tile for place in range(depths)]
        for tile in range(2 * chips)
    ]
    parts = redistribute(parts, ("depth", "chip", "core"), groups)
    return jnp.sum(parts, axis=0)


def solution(mesh):
    depths, tiles = mesh.devices.shape
    split_mesh = jax.sharding.Mesh(
        mesh.devices.reshape(depths, tiles // 2, 2), ("depth", "chip", "core")
    )
    rows = ("chip", "core")
    placed = (P("depth", rows, None), P(rows, None), P(rows, "depth"), P("depth"))
    return jax.shard_map(
        body, mesh=split_mesh, in_specs=placed, out_specs=P(rows, "depth"), check_vma=False
    )
```

```python
import numpy as np
import jax
import jax.numpy as jnp
import ml_dtypes
from jax import lax
from jax.experimental import pallas as pl
from jax.experimental.pallas import tpu as pltpu
from jax.sharding import PartitionSpec as P

PUPIL = 1024
HALF = 128
FREQ = 2 * HALF
GROUP = 16
GATHER_MASKS = (0, 2, 1, 3, 6, 4, 7, 5)
CHIPS = tuple(8 * y + z for z in reversed(range(8)) for y in (1, 0))
CHIP_ORDERS = (CHIPS, CHIPS[8:] + CHIPS[:8])
TILE_ORDER = tuple(2 * chip + core for chip in CHIPS for core in (1, 0))
EVEN, ODD = (0, 2, 4, 6), (1, 3, 5, 7)
WINDOW = FREQ + GROUP
defocus_step = 0.5


def split_table(table):
    high = table.astype(ml_dtypes.bfloat16)
    return high, (table - high.astype(np.float64)).astype(ml_dtypes.bfloat16)


def freq_tables():
    waves = np.arange(FREQ, dtype=np.int64) - HALF
    angle = (waves[:, None] * np.arange(PUPIL)[None, :]) % PUPIL * (2 * np.pi / PUPIL)
    cos, sin = np.cos(angle) * PUPIL**-0.5, -np.sin(angle) * PUPIL**-0.5
    gather = split_table(np.concatenate([cos.T, sin.T], axis=1))
    spread = split_table(np.concatenate([cos, sin], axis=1))
    half, place, row = np.indices((2, len(TILE_ORDER), 4)).reshape(3, -1)
    tile = np.array(TILE_ORDER)[place]
    owned = np.argsort(CHIP_ORDERS, axis=1)[tile % 2, tile // 2]
    arrived = 128 * (tile % 2) + 8 * owned + 4 * half + row
    return gather, spread, [part[arrived] for part in spread]


def split(x):
    high = x.astype(jnp.bfloat16)
    return high, (x - high.astype(jnp.float32)).astype(jnp.bfloat16)


def dot(left, right):
    return jnp.dot(left, right, preferred_element_type=jnp.float32)


def dot3(left, high_ref, low_ref):
    rows = left.shape[0]
    high, low = split(left)
    both = dot(jnp.concatenate([high, low], axis=0), high_ref[...])
    return both[:rows] + both[rows:] + dot(high, low_ref[...])


def shift_kernel(grad, shifts):
    tile_rows = shifts.shape[0] * GROUP
    row = lax.broadcasted_iota(jnp.int32, (tile_rows, FREQ), 0)
    lane = lax.broadcasted_iota(jnp.int32, (tile_rows, FREQ), 1)
    lane_bits = lax.broadcasted_iota(jnp.int32, (WINDOW, FREQ), 1)
    below = jnp.zeros((WINDOW - FREQ, FREQ), jnp.float32)
    columns = grad[...].astype(jnp.float32).T.astype(jnp.bfloat16)
    for step in range(tile_rows // GROUP):
        pick = jnp.where(row == GROUP * step + lane // GROUP, 1.0, 0.0).astype(jnp.bfloat16)
        moved = jnp.concatenate([dot(columns, pick), below], axis=0)
        for shift in (8, 4, 2, 1):
            moved = jnp.where(lane_bits & shift != 0, pltpu.roll(moved, shift, 0), moved)
        shifts[step, :HALF] = jnp.zeros((HALF, FREQ), jnp.bfloat16)
        shifts[step, HALF : HALF + WINDOW] = moved.astype(jnp.bfloat16)
        shifts[step, HALF + WINDOW :] = jnp.zeros((HALF - GROUP, FREQ), jnp.bfloat16)


def windows(core, near, far, own, ext, win):
    tile_rows = near.shape[0]
    here = core == 0
    ext[:tile_rows] = jnp.where(here, far[...], near[...])
    ext[tile_rows : 2 * tile_rows] = own[...]
    ext[2 * tile_rows :] = jnp.where(here, near[...], far[...])
    for step in range(tile_rows // GROUP):
        win[:, FREQ * step : FREQ * (step + 1)] = ext[GROUP * step : GROUP * step + WINDOW]


def exchanged(x, lane, width):
    left, right = pltpu.roll(x, HALF - width, 1), pltpu.roll(x, width, 1)
    return jnp.where(lane & width == 0, left, right)


def lags(win, shifts, half, places):
    lane = lax.broadcasted_iota(jnp.int32, (WINDOW - 8, HALF), 1)

    def raw(place):
        first = pl.multiple_of(FREQ - GROUP * place - HALF * half, GROUP)
        taps = shifts[:, pl.ds(first, FREQ), :].reshape(-1, FREQ)
        return dot(win[...], taps)

    def aligned(terms):
        part = terms[: WINDOW - 8, :HALF] + terms[8:, HALF:]
        for shift in (4, 2, 1):
            up = pltpu.roll(part, WINDOW - 8 - shift, 0)
            part = jnp.where(lane & (GROUP * shift) != 0, up, part)
        return part[:FREQ]

    parts, ahead = [], raw(places[0])
    for place in places[1:]:
        terms, ahead = ahead, raw(place)
        parts.append(aligned(terms))
    parts.append(aligned(ahead))
    lane = lax.broadcasted_iota(jnp.int32, (FREQ, HALF), 1)

    def merged(first, second, width):
        low = lane & width == 0
        rest = jnp.where(low, second, first)
        rest = pltpu.roll(rest, width, 1) if width == HALF // 2 else exchanged(rest, lane, width)
        return jnp.where(low, first, second) + rest

    both = merged(merged(parts[0], parts[2], 64), merged(parts[1], parts[3], 64), 32)
    return both + exchanged(both, lane, 16)


def interleaved(even, odd):
    lane = lax.broadcasted_iota(jnp.int32, (FREQ, HALF), 1)
    return jnp.where(lane & GROUP == 0, even, odd)


def by_owner(total):
    flipped = total.T.reshape(HALF // 8, 8, FREQ)
    return jnp.concatenate([flipped[:, :, :HALF], flipped[:, :, HALF:]], axis=1)


def first_kernel(core, far, near, own, shifts, win, even, ext):
    windows(core[0], near, far, own, ext, win)
    even[...] = lags(win, shifts, 1 - core[0], EVEN)


def second_kernel(core, win, shifts, even, out, kept):
    out[...] = by_owner(interleaved(even[...], lags(win, shifts, 1 - core[0], ODD)))
    kept[...] = lags(win, shifts, core[0], EVEN)


def third_kernel(core, win, shifts, kept, keep_z, out):
    out[:, :16] = by_owner(interleaved(kept[...], lags(win, shifts, core[0], ODD)))
    out[:, 16:] = keep_z[...]


def cos_sin(theta):
    turns = jnp.round(theta * (2 / np.pi))
    rest = theta - turns * 1.5703125
    rest = rest - turns * 4.837512969970703e-4
    rest = rest - turns * 7.549789948768648e-8
    square = rest * rest
    sin = rest + rest * square * (
        -1.6666654611e-1 + square * (8.3321608736e-3 + square * -1.9515295891e-4)
    )
    cos = (1.0 - 0.5 * square) + square * square * (
        4.166664568298827e-2 + square * (-1.388731625493765e-3 + square * 2.443315711809948e-5)
    )
    quarter = turns.astype(jnp.int32)
    odd = quarter & 1 != 0
    real, imag = jnp.where(odd, sin, cos), jnp.where(odd, cos, sin)
    real = jnp.where((quarter + 1) & 2 != 0, -real, real)
    imag = jnp.where(quarter & 2 != 0, -imag, imag)
    return real, imag


def field_kernel(
    first, depth, core, defocus, phase, send_k, high, low, keep, send, field_re, field_im, ordered
):
    blocks, rows, width = phase.shape
    for block in range(blocks):
        ordered[depth[0] ^ GATHER_MASKS[block]] = phase[block]
    full = jnp.concatenate([ordered[block] for block in range(blocks)], axis=1)
    centre = (PUPIL - 1) / 2.0
    shape = (rows, PUPIL)
    u = (lax.broadcasted_iota(jnp.int32, shape, 0) + first[0]).astype(jnp.float32)
    v = lax.broadcasted_iota(jnp.int32, shape, 1).astype(jnp.float32)
    radius = (u - centre) ** 2 + (v - centre) ** 2
    limit = (PUPIL / 2.0) ** 2
    inside = radius <= limit
    real, imag = cos_sin(full + defocus[0].astype(jnp.float32) * defocus_step * (radius / limit))
    real, imag = jnp.where(inside, real, 0.0), jnp.where(inside, imag, 0.0)
    field_re[...] = real
    field_im[...] = imag
    terms = dot3(jnp.concatenate([real, imag], axis=0), high, low)
    z_re = terms[:rows, :FREQ] - terms[rows:, FREQ:]
    z_im = terms[:rows, FREQ:] + terms[rows:, :FREQ]
    here = core[0] == 0
    blank = jnp.zeros((rows, FREQ), jnp.float32)
    first_re, second_re = jnp.where(here, z_re, blank), jnp.where(here, blank, z_re)
    first_im, second_im = jnp.where(here, z_im, blank), jnp.where(here, blank, z_im)
    z = jnp.concatenate([first_re, second_re, first_im, second_im], axis=0).T
    z_low, z_high = z[:HALF], z[HALF:]
    keep[...] = jnp.where(here, z_low, z_high).reshape(keep.shape)
    send[:, :16] = send_k[...]
    send[:, 16:] = jnp.where(here, z_high, z_low).reshape(keep.shape)


def middle_kernel(core, payload, g_high, g_low, s_high, s_low, out):
    chips = payload.shape[0]
    rows = PUPIL // chips
    kernel_grad = payload[0, :16]
    for chip in range(1, chips):
        kernel_grad = kernel_grad + payload[chip, :16]
    kernel_grad = jnp.concatenate([kernel_grad[:8], kernel_grad[8:]], axis=1)
    blocks = [[payload[order.index(chip), 16:] for order in CHIP_ORDERS] for chip in range(chips)]
    blocks = [jnp.where(core[0] == 0, *pair) for pair in blocks]
    z_re = jnp.concatenate([block[:, :rows] for block in blocks], axis=1)
    z_im = jnp.concatenate([block[:, rows:] for block in blocks], axis=1)
    terms = dot3(jnp.concatenate([z_re, z_im], axis=0), g_high, g_low)
    y_re = terms[:8, :FREQ] - terms[8:, FREQ:]
    y_im = terms[:8, FREQ:] + terms[8:, :FREQ]
    gy = 2.0 * jnp.concatenate([kernel_grad * y_re, kernel_grad * y_im], axis=0)
    terms = dot3(gy, s_high, s_low)
    gz_re = terms[:8, :PUPIL] + terms[8:, PUPIL:]
    gz_im = terms[8:, :PUPIL] - terms[:8, PUPIL:]
    rows = rows // 2
    for tile in range(2 * chips):
        here = slice(rows * tile, rows * (tile + 1))
        parts = [part[:, here] for part in (gz_re, gz_im)]
        rows_of = [part[half : half + 4] for half in (0, 4) for part in parts]
        out[TILE_ORDER.index(tile)] = jnp.concatenate(rows_of, axis=1)


def phase_kernel(payload, field_re, field_im, high, low, out):
    rows = field_re.shape[0]
    gz = payload[...].T
    gz_re = jnp.concatenate([gz[:rows], gz[2 * rows : 3 * rows]], axis=1)
    gz_im = jnp.concatenate([gz[rows : 2 * rows], gz[3 * rows :]], axis=1)
    terms = dot3(jnp.concatenate([gz_re, gz_im], axis=0), high, low)
    ge_re = terms[:rows, :PUPIL] + terms[rows:, PUPIL:]
    ge_im = terms[rows:, :PUPIL] - terms[:rows, PUPIL:]
    phase = field_re[...] * ge_im - field_im[...] * ge_re
    width = out.shape[2]
    for block in range(out.shape[0]):
        out[out.shape[0] - 1 - block] = phase[:, width * block : width * (block + 1)]


def call(kernel, outs, scratch, flops, moved, smem=0):
    def run(*args):
        spaces = [pltpu.SMEM if place < smem else pltpu.VMEM for place in range(len(args))]
        return pl.pallas_call(
            kernel,
            out_shape=outs,
            in_specs=[pl.BlockSpec(memory_space=space) for space in spaces],
            out_specs=jax.tree.map(lambda _: pl.BlockSpec(memory_space=pltpu.VMEM), outs),
            scratch_shapes=scratch,
            compiler_params=pltpu.CompilerParams(vmem_limit_bytes=40 * 2**20),
            cost_estimate=pl.CostEstimate(flops=flops, bytes_accessed=moved, transcendentals=0),
        )(*args)

    return run


def over_depth(x, mask):
    count = lax.axis_size("depth")
    return lax.ppermute(x, "depth", [(i, i ^ mask) for i in range(count)])


def beside(x, tiles):
    pairs = [(i, i + 1) for i in range(1, tiles - 1, 2)]
    return lax.ppermute(x, ("chip", "core"), pairs + [(j, i) for i, j in pairs])


def redistribute(x, axis, groups):
    return lax.all_to_all(x, axis, 0, 0, tiled=True, axis_index_groups=groups)


def swap(x):
    return lax.ppermute(x, "core", [(0, 1), (1, 0)])


def body(scene_layers, sensor_grad, pupil_phase, defocus_index):
    chips, depths = lax.axis_size("chip"), lax.axis_size("depth")
    rows, width = pupil_phase.shape
    f32 = jnp.float32
    (g_high, g_low), (s_high, s_low), (r_high, r_low) = freq_tables()
    core, depth, first_row = (
        lax.axis_index(axis).astype(jnp.int32)[None] for axis in ("core", "depth", ("chip", "core"))
    )
    first_row = first_row * rows
    scene = scene_layers[0]
    steps = scene.shape[0] // GROUP
    work = 2 * steps * FREQ * WINDOW * FREQ
    far = beside(scene, 2 * chips)
    other = over_depth(pupil_phase, GATHER_MASKS[1])
    shape, bf16 = jax.ShapeDtypeStruct, jnp.bfloat16
    shifts = call(
        shift_kernel,
        shape((steps, 2 * FREQ, FREQ), bf16),
        [],
        2 * scene.shape[0] * FREQ * FREQ * GROUP,
        2**22,
    )(sensor_grad)
    other, shifts, edge = lax.optimization_barrier((other, shifts, scene))
    near = swap(edge)
    gathered = jnp.stack([pupil_phase, other])
    beyond = over_depth(gathered, GATHER_MASKS[2])
    far, near, shifts = lax.optimization_barrier((far, near, shifts))
    lanes = shape((FREQ, HALF), f32)
    win, even = call(
        first_kernel,
        (shape((WINDOW, steps * FREQ), bf16), lanes),
        [pltpu.VMEM((3 * scene.shape[0], FREQ), bf16)],
        4 * work,
        2**19,
        smem=1,
    )(core, far, near, scene, shifts)
    beyond, win, even = lax.optimization_barrier((beyond, win, even))
    gathered = jnp.concatenate([gathered, beyond], axis=0)
    beyond = over_depth(gathered, GATHER_MASKS[4])
    send_k, even = call(
        second_kernel, (shape((chips, 16, HALF), f32), lanes), [], 8 * work, 2**19, smem=1
    )(core, win, shifts, even)
    beyond, send_k, even = lax.optimization_barrier((beyond, send_k, even))
    gathered = jnp.concatenate([gathered, beyond], axis=0)
    piece, both = shape((chips, 8, HALF), f32), shape((chips, 24, HALF), f32)
    field = shape((rows, PUPIL), f32)
    keep_z, send, field_re, field_im = call(
        field_kernel,
        (piece, both, field, field),
        [pltpu.VMEM((depths, rows, width), f32)],
        2 * 192 * PUPIL * 2 * FREQ,
        3 * 2**20,
        smem=4,
    )(first_row, depth, core, defocus_index, gathered, send_k, g_high, g_low)
    send, win = lax.optimization_barrier((send, win))
    other = swap(send)
    keep = call(third_kernel, both, [], 4 * work, 2**19, smem=1)(core, win, shifts, even, keep_z)
    other, keep = lax.optimization_barrier((other, keep))
    groups = [[2 * chip + place for chip in CHIP_ORDERS[place]] for place in range(2)]
    payload = redistribute(keep + other, ("chip", "core"), groups)
    payload = call(
        middle_kernel,
        jax.ShapeDtypeStruct((2 * chips, 4, HALF), f32),
        [],
        2 * 96 * PUPIL * 2 * FREQ,
        5 * 2**20,
        smem=1,
    )(core, payload, g_high, g_low, s_high, s_low)
    payload = redistribute(payload, ("chip", "core"), [list(TILE_ORDER)])
    parts = call(
        phase_kernel,
        jax.ShapeDtypeStruct((depths, rows, width), f32),
        [],
        2 * 192 * PUPIL * 2 * FREQ,
        3 * 2**20,
    )(payload.reshape(HALF, HALF), field_re, field_im, r_high, r_low)
    groups = [list(reversed(range(depths)))]
    parts = redistribute(parts, "depth", groups)
    return jnp.sum(parts, axis=0)


def solution(mesh):
    depths, tiles = mesh.devices.shape
    split_mesh = jax.sharding.Mesh(
        mesh.devices.reshape(depths, tiles // 2, 2), ("depth", "chip", "core")
    )
    rows = ("chip", "core")
    placed = (P("depth", rows, None), P(rows, None), P(rows, "depth"), P("depth"))
    return jax.shard_map(
        body, mesh=split_mesh, in_specs=placed, out_specs=P(rows, "depth"), check_vma=False
    )
```

```python
import numpy as np
import jax
import jax.numpy as jnp
import ml_dtypes
from jax import lax
from jax.experimental import pallas as pl
from jax.experimental.pallas import tpu as pltpu
from jax.sharding import PartitionSpec as P

PUPIL = 1024
HALF = 128
FREQ = 2 * HALF
GROUP = 16
GATHER_MASKS = (0, 2, 1, 3, 6, 4, 7, 5)
CHIPS = tuple(8 * y + z for z in reversed(range(8)) for y in (1, 0))
CHIP_ORDERS = (CHIPS, CHIPS[8:] + CHIPS[:8])
TILE_ORDER = tuple(2 * chip + core for chip in CHIPS[:-2] for core in (1, 0)) + (1, 17, 0, 16)
EVEN, ODD = (0, 2, 4, 6), (1, 3, 5, 7)
WINDOW = FREQ + GROUP
defocus_step = 0.5


def split_table(table):
    high = table.astype(ml_dtypes.bfloat16)
    return high, (table - high.astype(np.float64)).astype(ml_dtypes.bfloat16)


def freq_tables():
    waves = np.arange(FREQ, dtype=np.int64) - HALF
    angle = (waves[:, None] * np.arange(PUPIL)[None, :]) % PUPIL * (2 * np.pi / PUPIL)
    cos, sin = np.cos(angle) * PUPIL**-0.5, -np.sin(angle) * PUPIL**-0.5
    gather = split_table(np.concatenate([cos.T, sin.T], axis=1))
    spread = split_table(np.concatenate([cos, sin], axis=1))
    half, place, row = np.indices((2, len(TILE_ORDER), 4)).reshape(3, -1)
    tile = np.array(TILE_ORDER)[place]
    owned = np.argsort(CHIP_ORDERS, axis=1)[tile % 2, tile // 2]
    arrived = 128 * (tile % 2) + 8 * owned + 4 * half + row
    return gather, spread, [part[arrived] for part in spread]


def split(x):
    high = x.astype(jnp.bfloat16)
    return high, (x - high.astype(jnp.float32)).astype(jnp.bfloat16)


def dot(left, right):
    return jnp.dot(left, right, preferred_element_type=jnp.float32)


def dot3(left, high_ref, low_ref):
    rows = left.shape[0]
    high, low = split(left)
    both = dot(jnp.concatenate([high, low], axis=0), high_ref[...])
    return both[:rows] + both[rows:] + dot(high, low_ref[...])


def shift_kernel(grad, shifts):
    tile_rows = shifts.shape[0] * GROUP
    row = lax.broadcasted_iota(jnp.int32, (tile_rows, FREQ), 0)
    lane = lax.broadcasted_iota(jnp.int32, (tile_rows, FREQ), 1)
    lane_bits = lax.broadcasted_iota(jnp.int32, (WINDOW, FREQ), 1)
    below = jnp.zeros((WINDOW - FREQ, FREQ), jnp.float32)
    columns = grad[...].astype(jnp.float32).T.astype(jnp.bfloat16)
    for step in range(tile_rows // GROUP):
        pick = jnp.where(row == GROUP * step + lane // GROUP, 1.0, 0.0).astype(jnp.bfloat16)
        moved = jnp.concatenate([dot(columns, pick), below], axis=0)
        for shift in (8, 4, 2, 1):
            moved = jnp.where(lane_bits & shift != 0, pltpu.roll(moved, shift, 0), moved)
        shifts[step, :HALF] = jnp.zeros((HALF, FREQ), jnp.bfloat16)
        shifts[step, HALF : HALF + WINDOW] = moved.astype(jnp.bfloat16)
        shifts[step, HALF + WINDOW :] = jnp.zeros((HALF - GROUP, FREQ), jnp.bfloat16)


def windows(core, near, far, own, ext, win):
    tile_rows = near.shape[0]
    here = core == 0
    ext[:tile_rows] = jnp.where(here, far[...], near[...])
    ext[tile_rows : 2 * tile_rows] = own[...]
    ext[2 * tile_rows :] = jnp.where(here, near[...], far[...])
    for step in range(tile_rows // GROUP):
        win[:, FREQ * step : FREQ * (step + 1)] = ext[GROUP * step : GROUP * step + WINDOW]


def exchanged(x, lane, width):
    left, right = pltpu.roll(x, HALF - width, 1), pltpu.roll(x, width, 1)
    return jnp.where(lane & width == 0, left, right)


def lags(win, shifts, half, places):
    lane = lax.broadcasted_iota(jnp.int32, (WINDOW - 8, HALF), 1)

    def raw(place):
        first = pl.multiple_of(FREQ - GROUP * place - HALF * half, GROUP)
        taps = shifts[:, pl.ds(first, FREQ), :].reshape(-1, FREQ)
        return dot(win[...], taps)

    def aligned(terms):
        part = terms[: WINDOW - 8, :HALF] + terms[8:, HALF:]
        for shift in (4, 2, 1):
            up = pltpu.roll(part, WINDOW - 8 - shift, 0)
            part = jnp.where(lane & (GROUP * shift) != 0, up, part)
        return part[:FREQ]

    parts, ahead = [], raw(places[0])
    for place in places[1:]:
        terms, ahead = ahead, raw(place)
        parts.append(aligned(terms))
    parts.append(aligned(ahead))
    lane = lax.broadcasted_iota(jnp.int32, (FREQ, HALF), 1)

    def merged(first, second, width):
        low = lane & width == 0
        rest = jnp.where(low, second, first)
        rest = pltpu.roll(rest, width, 1) if width == HALF // 2 else exchanged(rest, lane, width)
        return jnp.where(low, first, second) + rest

    both = merged(merged(parts[0], parts[2], 64), merged(parts[1], parts[3], 64), 32)
    return both + exchanged(both, lane, 16)


def interleaved(even, odd):
    lane = lax.broadcasted_iota(jnp.int32, (FREQ, HALF), 1)
    return jnp.where(lane & GROUP == 0, even, odd)


def by_owner(total):
    flipped = total.T.reshape(HALF // 8, 8, FREQ)
    return jnp.concatenate([flipped[:, :, :HALF], flipped[:, :, HALF:]], axis=1)


def first_kernel(core, far, near, own, shifts, win, even, ext):
    windows(core[0], near, far, own, ext, win)
    even[...] = lags(win, shifts, 1 - core[0], EVEN)


def second_kernel(core, win, shifts, even, out, kept):
    out[...] = by_owner(interleaved(even[...], lags(win, shifts, 1 - core[0], ODD)))
    kept[...] = lags(win, shifts, core[0], EVEN)


def third_kernel(core, win, shifts, kept, keep_z, out):
    out[:, :16] = by_owner(interleaved(kept[...], lags(win, shifts, core[0], ODD)))
    out[:, 16:] = keep_z[...]


def cos_sin(theta):
    turns = jnp.round(theta * (2 / np.pi))
    rest = theta - turns * 1.5703125
    rest = rest - turns * 4.837512969970703e-4
    rest = rest - turns * 7.549789948768648e-8
    square = rest * rest
    sin = rest + rest * square * (
        -1.6666654611e-1 + square * (8.3321608736e-3 + square * -1.9515295891e-4)
    )
    cos = (1.0 - 0.5 * square) + square * square * (
        4.166664568298827e-2 + square * (-1.388731625493765e-3 + square * 2.443315711809948e-5)
    )
    quarter = turns.astype(jnp.int32)
    odd = quarter & 1 != 0
    real, imag = jnp.where(odd, sin, cos), jnp.where(odd, cos, sin)
    real = jnp.where((quarter + 1) & 2 != 0, -real, real)
    imag = jnp.where(quarter & 2 != 0, -imag, imag)
    return real, imag


def field_kernel(
    first, depth, core, defocus, phase, send_k, high, low, keep, send, field_re, field_im, ordered
):
    blocks, rows, width = phase.shape
    for block in range(blocks):
        ordered[depth[0] ^ GATHER_MASKS[block]] = phase[block]
    full = jnp.concatenate([ordered[block] for block in range(blocks)], axis=1)
    centre = (PUPIL - 1) / 2.0
    shape = (rows, PUPIL)
    u = (lax.broadcasted_iota(jnp.int32, shape, 0) + first[0]).astype(jnp.float32)
    v = lax.broadcasted_iota(jnp.int32, shape, 1).astype(jnp.float32)
    radius = (u - centre) ** 2 + (v - centre) ** 2
    limit = (PUPIL / 2.0) ** 2
    inside = radius <= limit
    real, imag = cos_sin(full + defocus[0].astype(jnp.float32) * defocus_step * (radius / limit))
    real, imag = jnp.where(inside, real, 0.0), jnp.where(inside, imag, 0.0)
    field_re[...] = real
    field_im[...] = imag
    terms = dot3(jnp.concatenate([real, imag], axis=0), high, low)
    z_re = terms[:rows, :FREQ] - terms[rows:, FREQ:]
    z_im = terms[:rows, FREQ:] + terms[rows:, :FREQ]
    here = core[0] == 0
    blank = jnp.zeros((rows, FREQ), jnp.float32)
    first_re, second_re = jnp.where(here, z_re, blank), jnp.where(here, blank, z_re)
    first_im, second_im = jnp.where(here, z_im, blank), jnp.where(here, blank, z_im)
    z = jnp.concatenate([first_re, second_re, first_im, second_im], axis=0).T
    z_low, z_high = z[:HALF], z[HALF:]
    keep[...] = jnp.where(here, z_low, z_high).reshape(keep.shape)
    send[:, :16] = send_k[...]
    send[:, 16:] = jnp.where(here, z_high, z_low).reshape(keep.shape)


def middle_kernel(core, payload, g_high, g_low, s_high, s_low, out):
    chips = payload.shape[0]
    rows = PUPIL // chips
    kernel_grad = payload[0, :16]
    for chip in range(1, chips):
        kernel_grad = kernel_grad + payload[chip, :16]
    kernel_grad = jnp.concatenate([kernel_grad[:8], kernel_grad[8:]], axis=1)
    blocks = [[payload[order.index(chip), 16:] for order in CHIP_ORDERS] for chip in range(chips)]
    blocks = [jnp.where(core[0] == 0, *pair) for pair in blocks]
    z_re = jnp.concatenate([block[:, :rows] for block in blocks], axis=1)
    z_im = jnp.concatenate([block[:, rows:] for block in blocks], axis=1)
    terms = dot3(jnp.concatenate([z_re, z_im], axis=0), g_high, g_low)
    y_re = terms[:8, :FREQ] - terms[8:, FREQ:]
    y_im = terms[:8, FREQ:] + terms[8:, :FREQ]
    gy = 2.0 * jnp.concatenate([kernel_grad * y_re, kernel_grad * y_im], axis=0)
    terms = dot3(gy, s_high, s_low)
    gz_re = terms[:8, :PUPIL] + terms[8:, PUPIL:]
    gz_im = terms[8:, :PUPIL] - terms[:8, PUPIL:]
    rows = rows // 2
    for tile in range(2 * chips):
        here = slice(rows * tile, rows * (tile + 1))
        parts = [part[:, here] for part in (gz_re, gz_im)]
        rows_of = [part[half : half + 4] for half in (0, 4) for part in parts]
        out[TILE_ORDER.index(tile)] = jnp.concatenate(rows_of, axis=1)


def phase_kernel(payload, field_re, field_im, high, low, out):
    rows = field_re.shape[0]
    gz = payload[...].T
    gz_re = jnp.concatenate([gz[:rows], gz[2 * rows : 3 * rows]], axis=1)
    gz_im = jnp.concatenate([gz[rows : 2 * rows], gz[3 * rows :]], axis=1)
    terms = dot3(jnp.concatenate([gz_re, gz_im], axis=0), high, low)
    ge_re = terms[:rows, :PUPIL] + terms[rows:, PUPIL:]
    ge_im = terms[rows:, :PUPIL] - terms[:rows, PUPIL:]
    phase = field_re[...] * ge_im - field_im[...] * ge_re
    width = out.shape[2]
    for block in range(out.shape[0]):
        out[out.shape[0] - 1 - block] = phase[:, width * block : width * (block + 1)]


def call(kernel, outs, scratch, flops, moved, smem=0):
    def run(*args):
        spaces = [pltpu.SMEM if place < smem else pltpu.VMEM for place in range(len(args))]
        return pl.pallas_call(
            kernel,
            out_shape=outs,
            in_specs=[pl.BlockSpec(memory_space=space) for space in spaces],
            out_specs=jax.tree.map(lambda _: pl.BlockSpec(memory_space=pltpu.VMEM), outs),
            scratch_shapes=scratch,
            compiler_params=pltpu.CompilerParams(vmem_limit_bytes=40 * 2**20),
            cost_estimate=pl.CostEstimate(flops=flops, bytes_accessed=moved, transcendentals=0),
        )(*args)

    return run


def over_depth(x, mask):
    count = lax.axis_size("depth")
    return lax.ppermute(x, "depth", [(i, i ^ mask) for i in range(count)])


def beside(x, tiles):
    pairs = [(i, i + 1) for i in range(1, tiles - 1, 2)]
    return lax.ppermute(x, ("chip", "core"), pairs + [(j, i) for i, j in pairs])


def redistribute(x, axis, groups):
    return lax.all_to_all(x, axis, 0, 0, tiled=True, axis_index_groups=groups)


def swap(x):
    return lax.ppermute(x, "core", [(0, 1), (1, 0)])


def body(scene_layers, sensor_grad, pupil_phase, defocus_index):
    chips, depths = lax.axis_size("chip"), lax.axis_size("depth")
    rows, width = pupil_phase.shape
    f32 = jnp.float32
    (g_high, g_low), (s_high, s_low), (r_high, r_low) = freq_tables()
    core, depth, first_row = (
        lax.axis_index(axis).astype(jnp.int32)[None] for axis in ("core", "depth", ("chip", "core"))
    )
    first_row = first_row * rows
    scene = scene_layers[0]
    steps = scene.shape[0] // GROUP
    work = 2 * steps * FREQ * WINDOW * FREQ
    far = beside(scene, 2 * chips)
    other = over_depth(pupil_phase, GATHER_MASKS[1])
    shape, bf16 = jax.ShapeDtypeStruct, jnp.bfloat16
    shifts = call(
        shift_kernel,
        shape((steps, 2 * FREQ, FREQ), bf16),
        [],
        2 * scene.shape[0] * FREQ * FREQ * GROUP,
        2**22,
    )(sensor_grad)
    other, shifts, edge = lax.optimization_barrier((other, shifts, scene))
    near = swap(edge)
    gathered = jnp.stack([pupil_phase, other])
    beyond = over_depth(gathered, GATHER_MASKS[2])
    far, near, shifts = lax.optimization_barrier((far, near, shifts))
    lanes = shape((FREQ, HALF), f32)
    win, even = call(
        first_kernel,
        (shape((WINDOW, steps * FREQ), bf16), lanes),
        [pltpu.VMEM((3 * scene.shape[0], FREQ), bf16)],
        4 * work,
        2**19,
        smem=1,
    )(core, far, near, scene, shifts)
    beyond, win, even = lax.optimization_barrier((beyond, win, even))
    gathered = jnp.concatenate([gathered, beyond], axis=0)
    beyond = over_depth(gathered, GATHER_MASKS[4])
    send_k, even = call(
        second_kernel, (shape((chips, 16, HALF), f32), lanes), [], 8 * work, 2**19, smem=1
    )(core, win, shifts, even)
    beyond, send_k, even = lax.optimization_barrier((beyond, send_k, even))
    gathered = jnp.concatenate([gathered, beyond], axis=0)
    piece, both = shape((chips, 8, HALF), f32), shape((chips, 24, HALF), f32)
    field = shape((rows, PUPIL), f32)
    keep_z, send, field_re, field_im = call(
        field_kernel,
        (piece, both, field, field),
        [pltpu.VMEM((depths, rows, width), f32)],
        2 * 192 * PUPIL * 2 * FREQ,
        3 * 2**20,
        smem=4,
    )(first_row, depth, core, defocus_index, gathered, send_k, g_high, g_low)
    send, win = lax.optimization_barrier((send, win))
    other = swap(send)
    keep = call(third_kernel, both, [], 4 * work, 2**19, smem=1)(core, win, shifts, even, keep_z)
    other, keep = lax.optimization_barrier((other, keep))
    groups = [[2 * chip + place for chip in CHIP_ORDERS[place]] for place in range(2)]
    payload = redistribute(keep + other, ("chip", "core"), groups)
    payload = call(
        middle_kernel,
        jax.ShapeDtypeStruct((2 * chips, 4, HALF), f32),
        [],
        2 * 96 * PUPIL * 2 * FREQ,
        5 * 2**20,
        smem=1,
    )(core, payload, g_high, g_low, s_high, s_low)
    payload = redistribute(payload, ("chip", "core"), [list(TILE_ORDER)])
    parts = call(
        phase_kernel,
        jax.ShapeDtypeStruct((depths, rows, width), f32),
        [],
        2 * 192 * PUPIL * 2 * FREQ,
        3 * 2**20,
    )(payload.reshape(HALF, HALF), field_re, field_im, r_high, r_low)
    groups = [list(reversed(range(depths)))]
    parts = redistribute(parts, "depth", groups)
    return jnp.sum(parts, axis=0)


def solution(mesh):
    depths, tiles = mesh.devices.shape
    split_mesh = jax.sharding.Mesh(
        mesh.devices.reshape(depths, tiles // 2, 2), ("depth", "chip", "core")
    )
    rows = ("chip", "core")
    placed = (P("depth", rows, None), P(rows, None), P(rows, "depth"), P("depth"))
    return jax.shard_map(
        body, mesh=split_mesh, in_specs=placed, out_specs=P(rows, "depth"), check_vma=False
    )
```

```python
import numpy as np
import jax
import jax.numpy as jnp
import ml_dtypes
from jax import lax
from jax.experimental import pallas as pl
from jax.experimental.pallas import tpu as pltpu
from jax.sharding import PartitionSpec as P

PUPIL = 1024
HALF = 128
FREQ = 2 * HALF
GROUP = 16
GATHER_MASKS = (0, 2, 1, 3, 6, 4, 7, 5)
CHIPS = tuple(8 * y + z for z in reversed(range(8)) for y in (1, 0))
FLIPPED = tuple(chip ^ 8 for chip in CHIPS)
CHIP_ORDERS = (FLIPPED, FLIPPED[8:] + FLIPPED[:8])
TILE_ORDER = tuple(2 * chip + core for chip in CHIPS for core in (1, 0))
EVEN, ODD = (0, 2, 4, 6), (1, 3, 5, 7)
WINDOW = FREQ + GROUP
defocus_step = 0.5


def split_table(table):
    high = table.astype(ml_dtypes.bfloat16)
    return high, (table - high.astype(np.float64)).astype(ml_dtypes.bfloat16)


def freq_tables():
    waves = np.arange(FREQ, dtype=np.int64) - HALF
    angle = (waves[:, None] * np.arange(PUPIL)[None, :]) % PUPIL * (2 * np.pi / PUPIL)
    cos, sin = np.cos(angle) * PUPIL**-0.5, -np.sin(angle) * PUPIL**-0.5
    gather = split_table(np.concatenate([cos.T, sin.T], axis=1))
    spread = split_table(np.concatenate([cos, sin], axis=1))
    half, place, row = np.indices((2, len(TILE_ORDER), 4)).reshape(3, -1)
    tile = np.array(TILE_ORDER)[place]
    owned = np.argsort(CHIP_ORDERS, axis=1)[tile % 2, tile // 2]
    arrived = 128 * (tile % 2) + 8 * owned + 4 * half + row
    return gather, spread, [part[arrived] for part in spread]


def split(x):
    high = x.astype(jnp.bfloat16)
    return high, (x - high.astype(jnp.float32)).astype(jnp.bfloat16)


def dot(left, right):
    return jnp.dot(left, right, preferred_element_type=jnp.float32)


def dot3(left, high_ref, low_ref):
    rows = left.shape[0]
    high, low = split(left)
    both = dot(jnp.concatenate([high, low], axis=0), high_ref[...])
    return both[:rows] + both[rows:] + dot(high, low_ref[...])


def shift_kernel(grad, shifts):
    tile_rows = shifts.shape[0] * GROUP
    row = lax.broadcasted_iota(jnp.int32, (tile_rows, FREQ), 0)
    lane = lax.broadcasted_iota(jnp.int32, (tile_rows, FREQ), 1)
    lane_bits = lax.broadcasted_iota(jnp.int32, (WINDOW, FREQ), 1)
    below = jnp.zeros((WINDOW - FREQ, FREQ), jnp.float32)
    columns = grad[...].astype(jnp.float32).T.astype(jnp.bfloat16)
    for step in range(tile_rows // GROUP):
        pick = jnp.where(row == GROUP * step + lane // GROUP, 1.0, 0.0).astype(jnp.bfloat16)
        moved = jnp.concatenate([dot(columns, pick), below], axis=0)
        for shift in (8, 4, 2, 1):
            moved = jnp.where(lane_bits & shift != 0, pltpu.roll(moved, shift, 0), moved)
        shifts[step, :HALF] = jnp.zeros((HALF, FREQ), jnp.bfloat16)
        shifts[step, HALF : HALF + WINDOW] = moved.astype(jnp.bfloat16)
        shifts[step, HALF + WINDOW :] = jnp.zeros((HALF - GROUP, FREQ), jnp.bfloat16)


def windows(core, near, far, own, ext, win):
    tile_rows = near.shape[0]
    here = core == 0
    ext[:tile_rows] = jnp.where(here, far[...], near[...])
    ext[tile_rows : 2 * tile_rows] = own[...]
    ext[2 * tile_rows :] = jnp.where(here, near[...], far[...])
    for step in range(tile_rows // GROUP):
        win[:, FREQ * step : FREQ * (step + 1)] = ext[GROUP * step : GROUP * step + WINDOW]


def exchanged(x, lane, width):
    left, right = pltpu.roll(x, HALF - width, 1), pltpu.roll(x, width, 1)
    return jnp.where(lane & width == 0, left, right)


def lags(win, shifts, half, places):
    lane = lax.broadcasted_iota(jnp.int32, (WINDOW - 8, HALF), 1)

    def raw(place):
        first = pl.multiple_of(FREQ - GROUP * place - HALF * half, GROUP)
        taps = shifts[:, pl.ds(first, FREQ), :].reshape(-1, FREQ)
        return dot(win[...], taps)

    def aligned(terms):
        part = terms[: WINDOW - 8, :HALF] + terms[8:, HALF:]
        for shift in (4, 2, 1):
            up = pltpu.roll(part, WINDOW - 8 - shift, 0)
            part = jnp.where(lane & (GROUP * shift) != 0, up, part)
        return part[:FREQ]

    parts, ahead = [], raw(places[0])
    for place in places[1:]:
        terms, ahead = ahead, raw(place)
        parts.append(aligned(terms))
    parts.append(aligned(ahead))
    lane = lax.broadcasted_iota(jnp.int32, (FREQ, HALF), 1)

    def merged(first, second, width):
        low = lane & width == 0
        rest = jnp.where(low, second, first)
        rest = pltpu.roll(rest, width, 1) if width == HALF // 2 else exchanged(rest, lane, width)
        return jnp.where(low, first, second) + rest

    both = merged(merged(parts[0], parts[2], 64), merged(parts[1], parts[3], 64), 32)
    return both + exchanged(both, lane, 16)


def interleaved(even, odd):
    lane = lax.broadcasted_iota(jnp.int32, (FREQ, HALF), 1)
    return jnp.where(lane & GROUP == 0, even, odd)


def by_owner(total):
    flipped = total.T.reshape(HALF // 8, 8, FREQ)
    return jnp.concatenate([flipped[:, :, :HALF], flipped[:, :, HALF:]], axis=1)


def first_kernel(core, far, near, own, shifts, win, even, ext):
    windows(core[0], near, far, own, ext, win)
    even[...] = lags(win, shifts, 1 - core[0], EVEN)


def second_kernel(core, win, shifts, even, out, kept):
    out[...] = by_owner(interleaved(even[...], lags(win, shifts, 1 - core[0], ODD)))
    kept[...] = lags(win, shifts, core[0], EVEN)


def third_kernel(core, win, shifts, kept, keep_z, out):
    out[:, :16] = by_owner(interleaved(kept[...], lags(win, shifts, core[0], ODD)))
    out[:, 16:] = keep_z[...]


def cos_sin(theta):
    turns = jnp.round(theta * (2 / np.pi))
    rest = theta - turns * 1.5703125
    rest = rest - turns * 4.837512969970703e-4
    rest = rest - turns * 7.549789948768648e-8
    square = rest * rest
    sin = rest + rest * square * (
        -1.6666654611e-1 + square * (8.3321608736e-3 + square * -1.9515295891e-4)
    )
    cos = (1.0 - 0.5 * square) + square * square * (
        4.166664568298827e-2 + square * (-1.388731625493765e-3 + square * 2.443315711809948e-5)
    )
    quarter = turns.astype(jnp.int32)
    odd = quarter & 1 != 0
    real, imag = jnp.where(odd, sin, cos), jnp.where(odd, cos, sin)
    real = jnp.where((quarter + 1) & 2 != 0, -real, real)
    imag = jnp.where(quarter & 2 != 0, -imag, imag)
    return real, imag


def field_kernel(
    first, depth, core, defocus, phase, send_k, high, low, keep, send, field_re, field_im, ordered
):
    blocks, rows, width = phase.shape
    for block in range(blocks):
        ordered[depth[0] ^ GATHER_MASKS[block]] = phase[block]
    full = jnp.concatenate([ordered[block] for block in range(blocks)], axis=1)
    centre = (PUPIL - 1) / 2.0
    shape = (rows, PUPIL)
    u = (lax.broadcasted_iota(jnp.int32, shape, 0) + first[0]).astype(jnp.float32)
    v = lax.broadcasted_iota(jnp.int32, shape, 1).astype(jnp.float32)
    radius = (u - centre) ** 2 + (v - centre) ** 2
    limit = (PUPIL / 2.0) ** 2
    inside = radius <= limit
    real, imag = cos_sin(full + defocus[0].astype(jnp.float32) * defocus_step * (radius / limit))
    real, imag = jnp.where(inside, real, 0.0), jnp.where(inside, imag, 0.0)
    field_re[...] = real
    field_im[...] = imag
    terms = dot3(jnp.concatenate([real, imag], axis=0), high, low)
    z_re = terms[:rows, :FREQ] - terms[rows:, FREQ:]
    z_im = terms[:rows, FREQ:] + terms[rows:, :FREQ]
    here = core[0] == 0
    blank = jnp.zeros((rows, FREQ), jnp.float32)
    first_re, second_re = jnp.where(here, z_re, blank), jnp.where(here, blank, z_re)
    first_im, second_im = jnp.where(here, z_im, blank), jnp.where(here, blank, z_im)
    z = jnp.concatenate([first_re, second_re, first_im, second_im], axis=0).T
    z_low, z_high = z[:HALF], z[HALF:]
    keep[...] = jnp.where(here, z_low, z_high).reshape(keep.shape)
    send[:, :16] = send_k[...]
    send[:, 16:] = jnp.where(here, z_high, z_low).reshape(keep.shape)


def middle_kernel(core, payload, g_high, g_low, s_high, s_low, out):
    chips = payload.shape[0]
    rows = PUPIL // chips
    kernel_grad = payload[0, :16]
    for chip in range(1, chips):
        kernel_grad = kernel_grad + payload[chip, :16]
    kernel_grad = jnp.concatenate([kernel_grad[:8], kernel_grad[8:]], axis=1)
    blocks = [[payload[order.index(chip), 16:] for order in CHIP_ORDERS] for chip in range(chips)]
    blocks = [jnp.where(core[0] == 0, *pair) for pair in blocks]
    z_re = jnp.concatenate([block[:, :rows] for block in blocks], axis=1)
    z_im = jnp.concatenate([block[:, rows:] for block in blocks], axis=1)
    terms = dot3(jnp.concatenate([z_re, z_im], axis=0), g_high, g_low)
    y_re = terms[:8, :FREQ] - terms[8:, FREQ:]
    y_im = terms[:8, FREQ:] + terms[8:, :FREQ]
    gy = 2.0 * jnp.concatenate([kernel_grad * y_re, kernel_grad * y_im], axis=0)
    terms = dot3(gy, s_high, s_low)
    gz_re = terms[:8, :PUPIL] + terms[8:, PUPIL:]
    gz_im = terms[8:, :PUPIL] - terms[:8, PUPIL:]
    rows = rows // 2
    for tile in range(2 * chips):
        here = slice(rows * tile, rows * (tile + 1))
        parts = [part[:, here] for part in (gz_re, gz_im)]
        rows_of = [part[half : half + 4] for half in (0, 4) for part in parts]
        out[TILE_ORDER.index(tile)] = jnp.concatenate(rows_of, axis=1)


def phase_kernel(payload, field_re, field_im, high, low, out):
    rows = field_re.shape[0]
    gz = payload[...].T
    gz_re = jnp.concatenate([gz[:rows], gz[2 * rows : 3 * rows]], axis=1)
    gz_im = jnp.concatenate([gz[rows : 2 * rows], gz[3 * rows :]], axis=1)
    terms = dot3(jnp.concatenate([gz_re, gz_im], axis=0), high, low)
    ge_re = terms[:rows, :PUPIL] + terms[rows:, PUPIL:]
    ge_im = terms[rows:, :PUPIL] - terms[:rows, PUPIL:]
    phase = field_re[...] * ge_im - field_im[...] * ge_re
    width = out.shape[2]
    for block in range(out.shape[0]):
        out[out.shape[0] - 1 - block] = phase[:, width * block : width * (block + 1)]


def call(kernel, outs, scratch, flops, moved, smem=0):
    def run(*args):
        spaces = [pltpu.SMEM if place < smem else pltpu.VMEM for place in range(len(args))]
        return pl.pallas_call(
            kernel,
            out_shape=outs,
            in_specs=[pl.BlockSpec(memory_space=space) for space in spaces],
            out_specs=jax.tree.map(lambda _: pl.BlockSpec(memory_space=pltpu.VMEM), outs),
            scratch_shapes=scratch,
            compiler_params=pltpu.CompilerParams(vmem_limit_bytes=40 * 2**20),
            cost_estimate=pl.CostEstimate(flops=flops, bytes_accessed=moved, transcendentals=0),
        )(*args)

    return run


def over_depth(x, mask):
    count = lax.axis_size("depth")
    return lax.ppermute(x, "depth", [(i, i ^ mask) for i in range(count)])


def beside(x, tiles):
    pairs = [(i, i + 1) for i in range(1, tiles - 1, 2)]
    return lax.ppermute(x, ("chip", "core"), pairs + [(j, i) for i, j in pairs])


def redistribute(x, axis, groups):
    return lax.all_to_all(x, axis, 0, 0, tiled=True, axis_index_groups=groups)


def swap(x):
    return lax.ppermute(x, "core", [(0, 1), (1, 0)])


def body(scene_layers, sensor_grad, pupil_phase, defocus_index):
    chips, depths = lax.axis_size("chip"), lax.axis_size("depth")
    rows, width = pupil_phase.shape
    f32 = jnp.float32
    (g_high, g_low), (s_high, s_low), (r_high, r_low) = freq_tables()
    core, depth, first_row = (
        lax.axis_index(axis).astype(jnp.int32)[None] for axis in ("core", "depth", ("chip", "core"))
    )
    first_row = first_row * rows
    scene = scene_layers[0]
    steps = scene.shape[0] // GROUP
    work = 2 * steps * FREQ * WINDOW * FREQ
    far = beside(scene, 2 * chips)
    other = over_depth(pupil_phase, GATHER_MASKS[1])
    shape, bf16 = jax.ShapeDtypeStruct, jnp.bfloat16
    shifts = call(
        shift_kernel,
        shape((steps, 2 * FREQ, FREQ), bf16),
        [],
        2 * scene.shape[0] * FREQ * FREQ * GROUP,
        2**22,
    )(sensor_grad)
    other, shifts, edge = lax.optimization_barrier((other, shifts, scene))
    near = swap(edge)
    gathered = jnp.stack([pupil_phase, other])
    beyond = over_depth(gathered, GATHER_MASKS[2])
    far, near, shifts = lax.optimization_barrier((far, near, shifts))
    lanes = shape((FREQ, HALF), f32)
    win, even = call(
        first_kernel,
        (shape((WINDOW, steps * FREQ), bf16), lanes),
        [pltpu.VMEM((3 * scene.shape[0], FREQ), bf16)],
        4 * work,
        2**19,
        smem=1,
    )(core, far, near, scene, shifts)
    beyond, win, even = lax.optimization_barrier((beyond, win, even))
    gathered = jnp.concatenate([gathered, beyond], axis=0)
    beyond = over_depth(gathered, GATHER_MASKS[4])
    send_k, even = call(
        second_kernel, (shape((chips, 16, HALF), f32), lanes), [], 8 * work, 2**19, smem=1
    )(core, win, shifts, even)
    beyond, send_k, even = lax.optimization_barrier((beyond, send_k, even))
    gathered = jnp.concatenate([gathered, beyond], axis=0)
    piece, both = shape((chips, 8, HALF), f32), shape((chips, 24, HALF), f32)
    field = shape((rows, PUPIL), f32)
    keep_z, send, field_re, field_im = call(
        field_kernel,
        (piece, both, field, field),
        [pltpu.VMEM((depths, rows, width), f32)],
        2 * 192 * PUPIL * 2 * FREQ,
        3 * 2**20,
        smem=4,
    )(first_row, depth, core, defocus_index, gathered, send_k, g_high, g_low)
    send, win = lax.optimization_barrier((send, win))
    other = swap(send)
    keep = call(third_kernel, both, [], 4 * work, 2**19, smem=1)(core, win, shifts, even, keep_z)
    other, keep = lax.optimization_barrier((other, keep))
    groups = [[2 * chip + place for chip in CHIP_ORDERS[place]] for place in range(2)]
    payload = redistribute(keep + other, ("chip", "core"), groups)
    payload = call(
        middle_kernel,
        jax.ShapeDtypeStruct((2 * chips, 4, HALF), f32),
        [],
        2 * 96 * PUPIL * 2 * FREQ,
        5 * 2**20,
        smem=1,
    )(core, payload, g_high, g_low, s_high, s_low)
    payload = redistribute(payload, ("chip", "core"), [list(TILE_ORDER)])
    parts = call(
        phase_kernel,
        jax.ShapeDtypeStruct((depths, rows, width), f32),
        [],
        2 * 192 * PUPIL * 2 * FREQ,
        3 * 2**20,
    )(payload.reshape(HALF, HALF), field_re, field_im, r_high, r_low)
    groups = [list(reversed(range(depths)))]
    parts = redistribute(parts, "depth", groups)
    return jnp.sum(parts, axis=0)


def solution(mesh):
    depths, tiles = mesh.devices.shape
    split_mesh = jax.sharding.Mesh(
        mesh.devices.reshape(depths, tiles // 2, 2), ("depth", "chip", "core")
    )
    rows = ("chip", "core")
    placed = (P("depth", rows, None), P(rows, None), P(rows, "depth"), P("depth"))
    return jax.shard_map(
        body, mesh=split_mesh, in_specs=placed, out_specs=P(rows, "depth"), check_vma=False
    )
```

```python
import numpy as np
import jax
import jax.numpy as jnp
import ml_dtypes
from jax import lax
from jax.experimental import pallas as pl
from jax.experimental.pallas import tpu as pltpu
from jax.sharding import PartitionSpec as P

PUPIL = 1024
HALF = 128
FREQ = 2 * HALF
GROUP = 16
GATHER_MASKS = (0, 2, 1, 3, 6, 4, 7, 5)
CHIPS = tuple(8 * y + z for z in reversed(range(8)) for y in (1, 0))
BY_HALF = tuple(reversed(range(16)))
CHIP_ORDERS = (BY_HALF, BY_HALF[8:] + BY_HALF[:8])
TILE_ORDER = tuple(2 * chip + core for chip in CHIPS for core in (1, 0))
EVEN, ODD = (0, 2, 4, 6), (1, 3, 5, 7)
WINDOW = FREQ + GROUP
defocus_step = 0.5


def split_table(table):
    high = table.astype(ml_dtypes.bfloat16)
    return high, (table - high.astype(np.float64)).astype(ml_dtypes.bfloat16)


def freq_tables():
    waves = np.arange(FREQ, dtype=np.int64) - HALF
    angle = (waves[:, None] * np.arange(PUPIL)[None, :]) % PUPIL * (2 * np.pi / PUPIL)
    cos, sin = np.cos(angle) * PUPIL**-0.5, -np.sin(angle) * PUPIL**-0.5
    gather = split_table(np.concatenate([cos.T, sin.T], axis=1))
    spread = split_table(np.concatenate([cos, sin], axis=1))
    half, place, row = np.indices((2, len(TILE_ORDER), 4)).reshape(3, -1)
    tile = np.array(TILE_ORDER)[place]
    owned = np.argsort(CHIP_ORDERS, axis=1)[tile % 2, tile // 2]
    arrived = 128 * (tile % 2) + 8 * owned + 4 * half + row
    return gather, spread, [part[arrived] for part in spread]


def split(x):
    high = x.astype(jnp.bfloat16)
    return high, (x - high.astype(jnp.float32)).astype(jnp.bfloat16)


def dot(left, right):
    return jnp.dot(left, right, preferred_element_type=jnp.float32)


def dot3(left, high_ref, low_ref):
    rows = left.shape[0]
    high, low = split(left)
    both = dot(jnp.concatenate([high, low], axis=0), high_ref[...])
    return both[:rows] + both[rows:] + dot(high, low_ref[...])


def shift_kernel(grad, shifts):
    tile_rows = shifts.shape[0] * GROUP
    row = lax.broadcasted_iota(jnp.int32, (tile_rows, FREQ), 0)
    lane = lax.broadcasted_iota(jnp.int32, (tile_rows, FREQ), 1)
    lane_bits = lax.broadcasted_iota(jnp.int32, (WINDOW, FREQ), 1)
    below = jnp.zeros((WINDOW - FREQ, FREQ), jnp.float32)
    columns = grad[...].astype(jnp.float32).T.astype(jnp.bfloat16)
    for step in range(tile_rows // GROUP):
        pick = jnp.where(row == GROUP * step + lane // GROUP, 1.0, 0.0).astype(jnp.bfloat16)
        moved = jnp.concatenate([dot(columns, pick), below], axis=0)
        for shift in (8, 4, 2, 1):
            moved = jnp.where(lane_bits & shift != 0, pltpu.roll(moved, shift, 0), moved)
        shifts[step, :HALF] = jnp.zeros((HALF, FREQ), jnp.bfloat16)
        shifts[step, HALF : HALF + WINDOW] = moved.astype(jnp.bfloat16)
        shifts[step, HALF + WINDOW :] = jnp.zeros((HALF - GROUP, FREQ), jnp.bfloat16)


def windows(core, near, far, own, ext, win):
    tile_rows = near.shape[0]
    here = core == 0
    ext[:tile_rows] = jnp.where(here, far[...], near[...])
    ext[tile_rows : 2 * tile_rows] = own[...]
    ext[2 * tile_rows :] = jnp.where(here, near[...], far[...])
    for step in range(tile_rows // GROUP):
        win[:, FREQ * step : FREQ * (step + 1)] = ext[GROUP * step : GROUP * step + WINDOW]


def exchanged(x, lane, width):
    left, right = pltpu.roll(x, HALF - width, 1), pltpu.roll(x, width, 1)
    return jnp.where(lane & width == 0, left, right)


def lags(win, shifts, half, places):
    lane = lax.broadcasted_iota(jnp.int32, (WINDOW - 8, HALF), 1)

    def raw(place):
        first = pl.multiple_of(FREQ - GROUP * place - HALF * half, GROUP)
        taps = shifts[:, pl.ds(first, FREQ), :].reshape(-1, FREQ)
        return dot(win[...], taps)

    def aligned(terms):
        part = terms[: WINDOW - 8, :HALF] + terms[8:, HALF:]
        for shift in (4, 2, 1):
            up = pltpu.roll(part, WINDOW - 8 - shift, 0)
            part = jnp.where(lane & (GROUP * shift) != 0, up, part)
        return part[:FREQ]

    parts, ahead = [], raw(places[0])
    for place in places[1:]:
        terms, ahead = ahead, raw(place)
        parts.append(aligned(terms))
    parts.append(aligned(ahead))
    lane = lax.broadcasted_iota(jnp.int32, (FREQ, HALF), 1)

    def merged(first, second, width):
        low = lane & width == 0
        rest = jnp.where(low, second, first)
        rest = pltpu.roll(rest, width, 1) if width == HALF // 2 else exchanged(rest, lane, width)
        return jnp.where(low, first, second) + rest

    both = merged(merged(parts[0], parts[2], 64), merged(parts[1], parts[3], 64), 32)
    return both + exchanged(both, lane, 16)


def interleaved(even, odd):
    lane = lax.broadcasted_iota(jnp.int32, (FREQ, HALF), 1)
    return jnp.where(lane & GROUP == 0, even, odd)


def by_owner(total):
    flipped = total.T.reshape(HALF // 8, 8, FREQ)
    return jnp.concatenate([flipped[:, :, :HALF], flipped[:, :, HALF:]], axis=1)


def first_kernel(core, far, near, own, shifts, win, even, ext):
    windows(core[0], near, far, own, ext, win)
    even[...] = lags(win, shifts, 1 - core[0], EVEN)


def second_kernel(core, win, shifts, even, out, kept):
    out[...] = by_owner(interleaved(even[...], lags(win, shifts, 1 - core[0], ODD)))
    kept[...] = lags(win, shifts, core[0], EVEN)


def third_kernel(core, win, shifts, kept, keep_z, out):
    out[:, :16] = by_owner(interleaved(kept[...], lags(win, shifts, core[0], ODD)))
    out[:, 16:] = keep_z[...]


def cos_sin(theta):
    turns = jnp.round(theta * (2 / np.pi))
    rest = theta - turns * 1.5703125
    rest = rest - turns * 4.837512969970703e-4
    rest = rest - turns * 7.549789948768648e-8
    square = rest * rest
    sin = rest + rest * square * (
        -1.6666654611e-1 + square * (8.3321608736e-3 + square * -1.9515295891e-4)
    )
    cos = (1.0 - 0.5 * square) + square * square * (
        4.166664568298827e-2 + square * (-1.388731625493765e-3 + square * 2.443315711809948e-5)
    )
    quarter = turns.astype(jnp.int32)
    odd = quarter & 1 != 0
    real, imag = jnp.where(odd, sin, cos), jnp.where(odd, cos, sin)
    real = jnp.where((quarter + 1) & 2 != 0, -real, real)
    imag = jnp.where(quarter & 2 != 0, -imag, imag)
    return real, imag


def field_kernel(
    first, depth, core, defocus, phase, send_k, high, low, keep, send, field_re, field_im, ordered
):
    blocks, rows, width = phase.shape
    for block in range(blocks):
        ordered[depth[0] ^ GATHER_MASKS[block]] = phase[block]
    full = jnp.concatenate([ordered[block] for block in range(blocks)], axis=1)
    centre = (PUPIL - 1) / 2.0
    shape = (rows, PUPIL)
    u = (lax.broadcasted_iota(jnp.int32, shape, 0) + first[0]).astype(jnp.float32)
    v = lax.broadcasted_iota(jnp.int32, shape, 1).astype(jnp.float32)
    radius = (u - centre) ** 2 + (v - centre) ** 2
    limit = (PUPIL / 2.0) ** 2
    inside = radius <= limit
    real, imag = cos_sin(full + defocus[0].astype(jnp.float32) * defocus_step * (radius / limit))
    real, imag = jnp.where(inside, real, 0.0), jnp.where(inside, imag, 0.0)
    field_re[...] = real
    field_im[...] = imag
    terms = dot3(jnp.concatenate([real, imag], axis=0), high, low)
    z_re = terms[:rows, :FREQ] - terms[rows:, FREQ:]
    z_im = terms[:rows, FREQ:] + terms[rows:, :FREQ]
    here = core[0] == 0
    blank = jnp.zeros((rows, FREQ), jnp.float32)
    first_re, second_re = jnp.where(here, z_re, blank), jnp.where(here, blank, z_re)
    first_im, second_im = jnp.where(here, z_im, blank), jnp.where(here, blank, z_im)
    z = jnp.concatenate([first_re, second_re, first_im, second_im], axis=0).T
    z_low, z_high = z[:HALF], z[HALF:]
    keep[...] = jnp.where(here, z_low, z_high).reshape(keep.shape)
    send[:, :16] = send_k[...]
    send[:, 16:] = jnp.where(here, z_high, z_low).reshape(keep.shape)


def middle_kernel(core, payload, g_high, g_low, s_high, s_low, out):
    chips = payload.shape[0]
    rows = PUPIL // chips
    kernel_grad = payload[0, :16]
    for chip in range(1, chips):
        kernel_grad = kernel_grad + payload[chip, :16]
    kernel_grad = jnp.concatenate([kernel_grad[:8], kernel_grad[8:]], axis=1)
    blocks = [[payload[order.index(chip), 16:] for order in CHIP_ORDERS] for chip in range(chips)]
    blocks = [jnp.where(core[0] == 0, *pair) for pair in blocks]
    z_re = jnp.concatenate([block[:, :rows] for block in blocks], axis=1)
    z_im = jnp.concatenate([block[:, rows:] for block in blocks], axis=1)
    terms = dot3(jnp.concatenate([z_re, z_im], axis=0), g_high, g_low)
    y_re = terms[:8, :FREQ] - terms[8:, FREQ:]
    y_im = terms[:8, FREQ:] + terms[8:, :FREQ]
    gy = 2.0 * jnp.concatenate([kernel_grad * y_re, kernel_grad * y_im], axis=0)
    terms = dot3(gy, s_high, s_low)
    gz_re = terms[:8, :PUPIL] + terms[8:, PUPIL:]
    gz_im = terms[8:, :PUPIL] - terms[:8, PUPIL:]
    rows = rows // 2
    for tile in range(2 * chips):
        here = slice(rows * tile, rows * (tile + 1))
        parts = [part[:, here] for part in (gz_re, gz_im)]
        rows_of = [part[half : half + 4] for half in (0, 4) for part in parts]
        out[TILE_ORDER.index(tile)] = jnp.concatenate(rows_of, axis=1)


def phase_kernel(payload, field_re, field_im, high, low, out):
    rows = field_re.shape[0]
    gz = payload[...].T
    gz_re = jnp.concatenate([gz[:rows], gz[2 * rows : 3 * rows]], axis=1)
    gz_im = jnp.concatenate([gz[rows : 2 * rows], gz[3 * rows :]], axis=1)
    terms = dot3(jnp.concatenate([gz_re, gz_im], axis=0), high, low)
    ge_re = terms[:rows, :PUPIL] + terms[rows:, PUPIL:]
    ge_im = terms[rows:, :PUPIL] - terms[:rows, PUPIL:]
    phase = field_re[...] * ge_im - field_im[...] * ge_re
    width = out.shape[2]
    for block in range(out.shape[0]):
        out[out.shape[0] - 1 - block] = phase[:, width * block : width * (block + 1)]


def call(kernel, outs, scratch, flops, moved, smem=0):
    def run(*args):
        spaces = [pltpu.SMEM if place < smem else pltpu.VMEM for place in range(len(args))]
        return pl.pallas_call(
            kernel,
            out_shape=outs,
            in_specs=[pl.BlockSpec(memory_space=space) for space in spaces],
            out_specs=jax.tree.map(lambda _: pl.BlockSpec(memory_space=pltpu.VMEM), outs),
            scratch_shapes=scratch,
            compiler_params=pltpu.CompilerParams(vmem_limit_bytes=40 * 2**20),
            cost_estimate=pl.CostEstimate(flops=flops, bytes_accessed=moved, transcendentals=0),
        )(*args)

    return run


def over_depth(x, mask):
    count = lax.axis_size("depth")
    return lax.ppermute(x, "depth", [(i, i ^ mask) for i in range(count)])


def beside(x, tiles):
    pairs = [(i, i + 1) for i in range(1, tiles - 1, 2)]
    return lax.ppermute(x, ("chip", "core"), pairs + [(j, i) for i, j in pairs])


def redistribute(x, axis, groups):
    return lax.all_to_all(x, axis, 0, 0, tiled=True, axis_index_groups=groups)


def swap(x):
    return lax.ppermute(x, "core", [(0, 1), (1, 0)])


def body(scene_layers, sensor_grad, pupil_phase, defocus_index):
    chips, depths = lax.axis_size("chip"), lax.axis_size("depth")
    rows, width = pupil_phase.shape
    f32 = jnp.float32
    (g_high, g_low), (s_high, s_low), (r_high, r_low) = freq_tables()
    core, depth, first_row = (
        lax.axis_index(axis).astype(jnp.int32)[None] for axis in ("core", "depth", ("chip", "core"))
    )
    first_row = first_row * rows
    scene = scene_layers[0]
    steps = scene.shape[0] // GROUP
    work = 2 * steps * FREQ * WINDOW * FREQ
    far = beside(scene, 2 * chips)
    other = over_depth(pupil_phase, GATHER_MASKS[1])
    shape, bf16 = jax.ShapeDtypeStruct, jnp.bfloat16
    shifts = call(
        shift_kernel,
        shape((steps, 2 * FREQ, FREQ), bf16),
        [],
        2 * scene.shape[0] * FREQ * FREQ * GROUP,
        2**22,
    )(sensor_grad)
    other, shifts, edge = lax.optimization_barrier((other, shifts, scene))
    near = swap(edge)
    gathered = jnp.stack([pupil_phase, other])
    beyond = over_depth(gathered, GATHER_MASKS[2])
    far, near, shifts = lax.optimization_barrier((far, near, shifts))
    lanes = shape((FREQ, HALF), f32)
    win, even = call(
        first_kernel,
        (shape((WINDOW, steps * FREQ), bf16), lanes),
        [pltpu.VMEM((3 * scene.shape[0], FREQ), bf16)],
        4 * work,
        2**19,
        smem=1,
    )(core, far, near, scene, shifts)
    beyond, win, even = lax.optimization_barrier((beyond, win, even))
    gathered = jnp.concatenate([gathered, beyond], axis=0)
    beyond = over_depth(gathered, GATHER_MASKS[4])
    send_k, even = call(
        second_kernel, (shape((chips, 16, HALF), f32), lanes), [], 8 * work, 2**19, smem=1
    )(core, win, shifts, even)
    beyond, send_k, even = lax.optimization_barrier((beyond, send_k, even))
    gathered = jnp.concatenate([gathered, beyond], axis=0)
    piece, both = shape((chips, 8, HALF), f32), shape((chips, 24, HALF), f32)
    field = shape((rows, PUPIL), f32)
    keep_z, send, field_re, field_im = call(
        field_kernel,
        (piece, both, field, field),
        [pltpu.VMEM((depths, rows, width), f32)],
        2 * 192 * PUPIL * 2 * FREQ,
        3 * 2**20,
        smem=4,
    )(first_row, depth, core, defocus_index, gathered, send_k, g_high, g_low)
    send, win = lax.optimization_barrier((send, win))
    other = swap(send)
    keep = call(third_kernel, both, [], 4 * work, 2**19, smem=1)(core, win, shifts, even, keep_z)
    other, keep = lax.optimization_barrier((other, keep))
    groups = [[2 * chip + place for chip in CHIP_ORDERS[place]] for place in range(2)]
    payload = redistribute(keep + other, ("chip", "core"), groups)
    payload = call(
        middle_kernel,
        jax.ShapeDtypeStruct((2 * chips, 4, HALF), f32),
        [],
        2 * 96 * PUPIL * 2 * FREQ,
        5 * 2**20,
        smem=1,
    )(core, payload, g_high, g_low, s_high, s_low)
    payload = redistribute(payload, ("chip", "core"), [list(TILE_ORDER)])
    parts = call(
        phase_kernel,
        jax.ShapeDtypeStruct((depths, rows, width), f32),
        [],
        2 * 192 * PUPIL * 2 * FREQ,
        3 * 2**20,
    )(payload.reshape(HALF, HALF), field_re, field_im, r_high, r_low)
    groups = [list(reversed(range(depths)))]
    parts = redistribute(parts, "depth", groups)
    return jnp.sum(parts, axis=0)


def solution(mesh):
    depths, tiles = mesh.devices.shape
    split_mesh = jax.sharding.Mesh(
        mesh.devices.reshape(depths, tiles // 2, 2), ("depth", "chip", "core")
    )
    rows = ("chip", "core")
    placed = (P("depth", rows, None), P(rows, None), P(rows, "depth"), P("depth"))
    return jax.shard_map(
        body, mesh=split_mesh, in_specs=placed, out_specs=P(rows, "depth"), check_vma=False
    )
```

```python
import numpy as np
import jax
import jax.numpy as jnp
import ml_dtypes
from jax import lax
from jax.experimental import pallas as pl
from jax.experimental.pallas import tpu as pltpu
from jax.sharding import PartitionSpec as P

PUPIL = 1024
HALF = 128
FREQ = 2 * HALF
GROUP = 16
GATHER_MASKS = (0, 2, 1, 3, 6, 4, 7, 5)
CHIP_ORDER = tuple(8 * y + z for z in reversed(range(8)) for y in (1, 0))
TILE_ORDER = tuple(2 * chip + core for chip in CHIP_ORDER for core in (1, 0))
DEPTH_ORDER = tuple(reversed(range(8)))
EVEN, ODD = (0, 2, 4, 6), (1, 3, 5, 7)
WINDOW = FREQ + GROUP
defocus_step = 0.5


def split_table(table):
    high = table.astype(ml_dtypes.bfloat16)
    return high, (table - high.astype(np.float64)).astype(ml_dtypes.bfloat16)


def freq_tables():
    waves = np.arange(FREQ, dtype=np.int64) - HALF
    angle = (waves[:, None] * np.arange(PUPIL)[None, :]) % PUPIL * (2 * np.pi / PUPIL)
    cos, sin = np.cos(angle) * PUPIL**-0.5, -np.sin(angle) * PUPIL**-0.5
    gather = split_table(np.concatenate([cos.T, sin.T], axis=1))
    spread = split_table(np.concatenate([cos, sin], axis=1))
    half, place, row = np.indices((2, len(TILE_ORDER), 4)).reshape(3, -1)
    tile = np.array(TILE_ORDER)[place]
    arrived = 128 * (tile % 2) + 8 * np.argsort(CHIP_ORDER)[tile // 2] + 4 * half + row
    return gather, spread, [part[arrived] for part in spread]


def split(x):
    high = x.astype(jnp.bfloat16)
    return high, (x - high.astype(jnp.float32)).astype(jnp.bfloat16)


def dot(left, right):
    return jnp.dot(left, right, preferred_element_type=jnp.float32)


def dot3(left, high_ref, low_ref):
    rows = left.shape[0]
    high, low = split(left)
    both = dot(jnp.concatenate([high, low], axis=0), high_ref[...])
    return both[:rows] + both[rows:] + dot(high, low_ref[...])


def shift_kernel(grad, shifts):
    tile_rows = shifts.shape[0] * GROUP
    row = lax.broadcasted_iota(jnp.int32, (tile_rows, FREQ), 0)
    lane = lax.broadcasted_iota(jnp.int32, (tile_rows, FREQ), 1)
    lane_bits = lax.broadcasted_iota(jnp.int32, (WINDOW, FREQ), 1)
    below = jnp.zeros((WINDOW - FREQ, FREQ), jnp.float32)
    columns = grad[...].astype(jnp.float32).T.astype(jnp.bfloat16)
    for step in range(tile_rows // GROUP):
        pick = jnp.where(row == GROUP * step + lane // GROUP, 1.0, 0.0).astype(jnp.bfloat16)
        moved = jnp.concatenate([dot(columns, pick), below], axis=0)
        for shift in (8, 4, 2, 1):
            moved = jnp.where(lane_bits & shift != 0, pltpu.roll(moved, shift, 0), moved)
        shifts[step, :HALF] = jnp.zeros((HALF, FREQ), jnp.bfloat16)
        shifts[step, HALF : HALF + WINDOW] = moved.astype(jnp.bfloat16)
        shifts[step, HALF + WINDOW :] = jnp.zeros((HALF - GROUP, FREQ), jnp.bfloat16)


def windows(core, near, far, own, ext, win):
    tile_rows = near.shape[0]
    here = core == 0
    ext[:tile_rows] = jnp.where(here, far[...], near[...])
    ext[tile_rows : 2 * tile_rows] = own[...]
    ext[2 * tile_rows :] = jnp.where(here, near[...], far[...])
    for step in range(tile_rows // GROUP):
        win[:, FREQ * step : FREQ * (step + 1)] = ext[GROUP * step : GROUP * step + WINDOW]


def exchanged(x, lane, width):
    left, right = pltpu.roll(x, HALF - width, 1), pltpu.roll(x, width, 1)
    return jnp.where(lane & width == 0, left, right)


def lags(win, shifts, half, places):
    lane = lax.broadcasted_iota(jnp.int32, (WINDOW - 8, HALF), 1)

    def raw(place):
        first = pl.multiple_of(FREQ - GROUP * place - HALF * half, GROUP)
        taps = shifts[:, pl.ds(first, FREQ), :].reshape(-1, FREQ)
        return dot(win[...], taps)

    def aligned(terms):
        part = terms[: WINDOW - 8, :HALF] + terms[8:, HALF:]
        for shift in (4, 2, 1):
            up = pltpu.roll(part, WINDOW - 8 - shift, 0)
            part = jnp.where(lane & (GROUP * shift) != 0, up, part)
        return part[:FREQ]

    parts, ahead = [], raw(places[0])
    for place in places[1:]:
        terms, ahead = ahead, raw(place)
        parts.append(aligned(terms))
    parts.append(aligned(ahead))
    lane = lax.broadcasted_iota(jnp.int32, (FREQ, HALF), 1)

    def merged(first, second, width):
        low = lane & width == 0
        rest = jnp.where(low, second, first)
        rest = pltpu.roll(rest, width, 1) if width == HALF // 2 else exchanged(rest, lane, width)
        return jnp.where(low, first, second) + rest

    both = merged(merged(parts[0], parts[2], 64), merged(parts[1], parts[3], 64), 32)
    return both + exchanged(both, lane, 16)


def interleaved(even, odd):
    lane = lax.broadcasted_iota(jnp.int32, (FREQ, HALF), 1)
    return jnp.where(lane & GROUP == 0, even, odd)


def by_owner(total):
    flipped = total.T.reshape(HALF // 8, 8, FREQ)
    return jnp.concatenate([flipped[:, :, :HALF], flipped[:, :, HALF:]], axis=1)


def first_kernel(core, far, near, own, shifts, win, even, ext):
    windows(core[0], near, far, own, ext, win)
    even[...] = lags(win, shifts, 1 - core[0], EVEN)


def second_kernel(core, win, shifts, even, out, kept):
    out[...] = by_owner(interleaved(even[...], lags(win, shifts, 1 - core[0], ODD)))
    kept[...] = lags(win, shifts, core[0], EVEN)


def third_kernel(core, win, shifts, kept, keep_z, out):
    out[:, :16] = by_owner(interleaved(kept[...], lags(win, shifts, core[0], ODD)))
    out[:, 16:] = keep_z[...]


def cos_sin(theta):
    turns = jnp.round(theta * (2 / np.pi))
    rest = theta - turns * 1.5703125
    rest = rest - turns * 4.837512969970703e-4
    rest = rest - turns * 7.549789948768648e-8
    square = rest * rest
    sin = rest + rest * square * (
        -1.6666654611e-1 + square * (8.3321608736e-3 + square * -1.9515295891e-4)
    )
    cos = (1.0 - 0.5 * square) + square * square * (
        4.166664568298827e-2 + square * (-1.388731625493765e-3 + square * 2.443315711809948e-5)
    )
    quarter = turns.astype(jnp.int32)
    odd = quarter & 1 != 0
    real, imag = jnp.where(odd, sin, cos), jnp.where(odd, cos, sin)
    real = jnp.where((quarter + 1) & 2 != 0, -real, real)
    imag = jnp.where(quarter & 2 != 0, -imag, imag)
    return real, imag


def field_kernel(
    first, depth, core, defocus, phase, send_k, high, low, keep, send, field_re, field_im, ordered
):
    blocks, rows, width = phase.shape
    for block in range(blocks):
        ordered[depth[0] ^ GATHER_MASKS[block]] = phase[block]
    full = jnp.concatenate([ordered[block] for block in range(blocks)], axis=1)
    centre = (PUPIL - 1) / 2.0
    shape = (rows, PUPIL)
    u = (lax.broadcasted_iota(jnp.int32, shape, 0) + first[0]).astype(jnp.float32)
    v = lax.broadcasted_iota(jnp.int32, shape, 1).astype(jnp.float32)
    radius = (u - centre) ** 2 + (v - centre) ** 2
    limit = (PUPIL / 2.0) ** 2
    inside = radius <= limit
    real, imag = cos_sin(full + defocus[0].astype(jnp.float32) * defocus_step * (radius / limit))
    real, imag = jnp.where(inside, real, 0.0), jnp.where(inside, imag, 0.0)
    field_re[...] = real
    field_im[...] = imag
    terms = dot3(jnp.concatenate([real, imag], axis=0), high, low)
    z_re = terms[:rows, :FREQ] - terms[rows:, FREQ:]
    z_im = terms[:rows, FREQ:] + terms[rows:, :FREQ]
    here = core[0] == 0
    blank = jnp.zeros((rows, FREQ), jnp.float32)
    first_re, second_re = jnp.where(here, z_re, blank), jnp.where(here, blank, z_re)
    first_im, second_im = jnp.where(here, z_im, blank), jnp.where(here, blank, z_im)
    z = jnp.concatenate([first_re, second_re, first_im, second_im], axis=0).T
    z_low, z_high = z[:HALF], z[HALF:]
    keep[...] = jnp.where(here, z_low, z_high).reshape(keep.shape)
    send[:, :16] = send_k[...]
    send[:, 16:] = jnp.where(here, z_high, z_low).reshape(keep.shape)


def middle_kernel(payload, g_high, g_low, s_high, s_low, out):
    chips = payload.shape[0]
    rows = PUPIL // chips
    kernel_grad = payload[0, :16]
    for chip in range(1, chips):
        kernel_grad = kernel_grad + payload[chip, :16]
    kernel_grad = jnp.concatenate([kernel_grad[:8], kernel_grad[8:]], axis=1)
    order = [CHIP_ORDER.index(chip) for chip in range(chips)]
    z_re = jnp.concatenate([payload[place, 16:, :rows] for place in order], axis=1)
    z_im = jnp.concatenate([payload[place, 16:, rows:] for place in order], axis=1)
    terms = dot3(jnp.concatenate([z_re, z_im], axis=0), g_high, g_low)
    y_re = terms[:8, :FREQ] - terms[8:, FREQ:]
    y_im = terms[:8, FREQ:] + terms[8:, :FREQ]
    gy = 2.0 * jnp.concatenate([kernel_grad * y_re, kernel_grad * y_im], axis=0)
    terms = dot3(gy, s_high, s_low)
    gz_re = terms[:8, :PUPIL] + terms[8:, PUPIL:]
    gz_im = terms[8:, :PUPIL] - terms[:8, PUPIL:]
    rows = rows // 2
    for tile in range(2 * chips):
        here = slice(rows * tile, rows * (tile + 1))
        parts = [part[:, here] for part in (gz_re, gz_im)]
        rows_of = [part[half : half + 4] for half in (0, 4) for part in parts]
        out[TILE_ORDER.index(tile)] = jnp.concatenate(rows_of, axis=1)


def phase_kernel(payload, field_re, field_im, high, low, out):
    rows = field_re.shape[0]
    gz = payload[...].T
    gz_re = jnp.concatenate([gz[:rows], gz[2 * rows : 3 * rows]], axis=1)
    gz_im = jnp.concatenate([gz[rows : 2 * rows], gz[3 * rows :]], axis=1)
    terms = dot3(jnp.concatenate([gz_re, gz_im], axis=0), high, low)
    ge_re = terms[:rows, :PUPIL] + terms[rows:, PUPIL:]
    ge_im = terms[rows:, :PUPIL] - terms[:rows, PUPIL:]
    phase = field_re[...] * ge_im - field_im[...] * ge_re
    width = out.shape[2]
    for block in range(out.shape[0]):
        out[DEPTH_ORDER.index(block)] = phase[:, width * block : width * (block + 1)]


def call(kernel, outs, scratch, flops, moved, smem=0):
    def run(*args):
        spaces = [pltpu.SMEM if place < smem else pltpu.VMEM for place in range(len(args))]
        return pl.pallas_call(
            kernel,
            out_shape=outs,
            in_specs=[pl.BlockSpec(memory_space=space) for space in spaces],
            out_specs=jax.tree.map(lambda _: pl.BlockSpec(memory_space=pltpu.VMEM), outs),
            scratch_shapes=scratch,
            compiler_params=pltpu.CompilerParams(vmem_limit_bytes=40 * 2**20),
            cost_estimate=pl.CostEstimate(flops=flops, bytes_accessed=moved, transcendentals=0),
        )(*args)

    return run


def over_depth(x, mask):
    count = lax.axis_size("depth")
    return lax.ppermute(x, "depth", [(i, i ^ mask) for i in range(count)])


def beside(x, tiles):
    pairs = [(i, i + 1) for i in range(1, tiles - 1, 2)]
    return lax.ppermute(x, ("chip", "core"), pairs + [(j, i) for i, j in pairs])


def redistribute(x, axis, order):
    return lax.all_to_all(x, axis, 0, 0, tiled=True, axis_index_groups=[list(order)])


def swap(x):
    return lax.ppermute(x, "core", [(0, 1), (1, 0)])


def body(scene_layers, sensor_grad, pupil_phase, defocus_index):
    chips, depths = lax.axis_size("chip"), lax.axis_size("depth")
    rows, width = pupil_phase.shape
    f32 = jnp.float32
    (g_high, g_low), (s_high, s_low), (r_high, r_low) = freq_tables()
    core, depth, first_row = (
        lax.axis_index(axis).astype(jnp.int32)[None] for axis in ("core", "depth", ("chip", "core"))
    )
    first_row = first_row * rows
    scene = scene_layers[0]
    steps = scene.shape[0] // GROUP
    work = 2 * steps * FREQ * WINDOW * FREQ
    far = beside(scene, 2 * chips)
    other = over_depth(pupil_phase, GATHER_MASKS[1])
    shape, bf16 = jax.ShapeDtypeStruct, jnp.bfloat16
    shifts = call(
        shift_kernel,
        shape((steps, 2 * FREQ, FREQ), bf16),
        [],
        2 * scene.shape[0] * FREQ * FREQ * GROUP,
        2**22,
    )(sensor_grad)
    other, shifts, edge, index = lax.optimization_barrier((other, shifts, scene, defocus_index))
    near = swap(edge)
    gathered = jnp.stack([pupil_phase, other])
    beyond = over_depth(gathered, GATHER_MASKS[2])
    far, near, shifts = lax.optimization_barrier((far, near, shifts))
    lanes = shape((FREQ, HALF), f32)
    win, even = call(
        first_kernel,
        (shape((WINDOW, steps * FREQ), bf16), lanes),
        [pltpu.VMEM((3 * scene.shape[0], FREQ), bf16)],
        4 * work,
        2**19,
        smem=1,
    )(core, far, near, scene, shifts)
    beyond, win, even = lax.optimization_barrier((beyond, win, even))
    gathered = jnp.concatenate([gathered, beyond], axis=0)
    beyond = over_depth(gathered, GATHER_MASKS[4])
    send_k, even = call(
        second_kernel, (shape((chips, 16, HALF), f32), lanes), [], 8 * work, 2**19, smem=1
    )(core, win, shifts, even)
    beyond, send_k, even = lax.optimization_barrier((beyond, send_k, even))
    gathered = jnp.concatenate([gathered, beyond], axis=0)
    piece, both = shape((chips, 8, HALF), f32), shape((chips, 24, HALF), f32)
    field = shape((rows, PUPIL), f32)
    keep_z, send, field_re, field_im = call(
        field_kernel,
        (piece, both, field, field),
        [pltpu.VMEM((depths, rows, width), f32)],
        2 * 192 * PUPIL * 2 * FREQ,
        3 * 2**20,
        smem=4,
    )(first_row, depth, core, index, gathered, send_k, g_high, g_low)
    send, win = lax.optimization_barrier((send, win))
    other = swap(send)
    keep = call(third_kernel, both, [], 4 * work, 2**19, smem=1)(core, win, shifts, even, keep_z)
    other, keep = lax.optimization_barrier((other, keep))
    payload = redistribute(keep + other, "chip", CHIP_ORDER)
    payload = call(
        middle_kernel,
        jax.ShapeDtypeStruct((2 * chips, 4, HALF), f32),
        [],
        2 * 96 * PUPIL * 2 * FREQ,
        5 * 2**20,
    )(payload, g_high, g_low, s_high, s_low)
    payload = redistribute(payload, ("chip", "core"), TILE_ORDER)
    parts = call(
        phase_kernel,
        jax.ShapeDtypeStruct((depths, rows, width), f32),
        [],
        2 * 192 * PUPIL * 2 * FREQ,
        3 * 2**20,
    )(payload.reshape(HALF, HALF), field_re, field_im, r_high, r_low)
    parts = redistribute(parts, "depth", DEPTH_ORDER)
    return jnp.sum(parts, axis=0)


def solution(mesh):
    depths, tiles = mesh.devices.shape
    split_mesh = jax.sharding.Mesh(
        mesh.devices.reshape(depths, tiles // 2, 2), ("depth", "chip", "core")
    )
    rows = ("chip", "core")
    placed = (P("depth", rows, None), P(rows, None), P(rows, "depth"), P("depth"))
    return jax.shard_map(
        body, mesh=split_mesh, in_specs=placed, out_specs=P(rows, "depth"), check_vma=False
    )
```

```python
import numpy as np
import jax
import jax.numpy as jnp
import ml_dtypes
from jax import lax
from jax.experimental import pallas as pl
from jax.experimental.pallas import tpu as pltpu
from jax.sharding import PartitionSpec as P

PUPIL = 1024
HALF = 128
FREQ = 2 * HALF
GROUP = 16
GATHER_MASKS = (0, 2, 1, 3, 6, 4, 7, 5)
CHIP_ORDER = tuple(reversed(range(16)))
TILE_ORDER = tuple(
    16 * y + 2 * z + core for z in reversed(range(8)) for y in (1, 0) for core in (1, 0)
)
DEPTH_ORDER = tuple(reversed(range(8)))
EVEN, ODD = (0, 2, 4, 6), (1, 3, 5, 7)
WINDOW = FREQ + GROUP
defocus_step = 0.5


def split_table(table):
    high = table.astype(ml_dtypes.bfloat16)
    return high, (table - high.astype(np.float64)).astype(ml_dtypes.bfloat16)


def freq_tables():
    waves = np.arange(FREQ, dtype=np.int64) - HALF
    angle = (waves[:, None] * np.arange(PUPIL)[None, :]) % PUPIL * (2 * np.pi / PUPIL)
    cos, sin = np.cos(angle) * PUPIL**-0.5, -np.sin(angle) * PUPIL**-0.5
    gather = split_table(np.concatenate([cos.T, sin.T], axis=1))
    spread = split_table(np.concatenate([cos, sin], axis=1))
    half, place, row = np.indices((2, len(TILE_ORDER), 4)).reshape(3, -1)
    tile = np.array(TILE_ORDER)[place]
    arrived = 128 * (tile % 2) + 8 * np.argsort(CHIP_ORDER)[tile // 2] + 4 * half + row
    return gather, spread, [part[arrived] for part in spread]


def split(x):
    high = x.astype(jnp.bfloat16)
    return high, (x - high.astype(jnp.float32)).astype(jnp.bfloat16)


def dot(left, right):
    return jnp.dot(left, right, preferred_element_type=jnp.float32)


def dot3(left, high_ref, low_ref):
    rows = left.shape[0]
    high, low = split(left)
    both = dot(jnp.concatenate([high, low], axis=0), high_ref[...])
    return both[:rows] + both[rows:] + dot(high, low_ref[...])


def shift_kernel(grad, shifts):
    tile_rows = shifts.shape[0] * GROUP
    row = lax.broadcasted_iota(jnp.int32, (tile_rows, FREQ), 0)
    lane = lax.broadcasted_iota(jnp.int32, (tile_rows, FREQ), 1)
    lane_bits = lax.broadcasted_iota(jnp.int32, (WINDOW, FREQ), 1)
    below = jnp.zeros((WINDOW - FREQ, FREQ), jnp.float32)
    columns = grad[...].astype(jnp.float32).T.astype(jnp.bfloat16)
    for step in range(tile_rows // GROUP):
        pick = jnp.where(row == GROUP * step + lane // GROUP, 1.0, 0.0).astype(jnp.bfloat16)
        moved = jnp.concatenate([dot(columns, pick), below], axis=0)
        for shift in (8, 4, 2, 1):
            moved = jnp.where(lane_bits & shift != 0, pltpu.roll(moved, shift, 0), moved)
        shifts[step, :HALF] = jnp.zeros((HALF, FREQ), jnp.bfloat16)
        shifts[step, HALF : HALF + WINDOW] = moved.astype(jnp.bfloat16)
        shifts[step, HALF + WINDOW :] = jnp.zeros((HALF - GROUP, FREQ), jnp.bfloat16)


def windows(core, near, far, own, ext, win):
    tile_rows = near.shape[0]
    here = core == 0
    ext[:tile_rows] = jnp.where(here, far[...], near[...])
    ext[tile_rows : 2 * tile_rows] = own[...]
    ext[2 * tile_rows :] = jnp.where(here, near[...], far[...])
    for step in range(tile_rows // GROUP):
        win[:, FREQ * step : FREQ * (step + 1)] = ext[GROUP * step : GROUP * step + WINDOW]


def exchanged(x, lane, width):
    left, right = pltpu.roll(x, HALF - width, 1), pltpu.roll(x, width, 1)
    return jnp.where(lane & width == 0, left, right)


def lags(win, shifts, half, places):
    lane = lax.broadcasted_iota(jnp.int32, (WINDOW - 8, HALF), 1)

    def raw(place):
        first = pl.multiple_of(FREQ - GROUP * place - HALF * half, GROUP)
        taps = shifts[:, pl.ds(first, FREQ), :].reshape(-1, FREQ)
        return dot(win[...], taps)

    def aligned(terms):
        part = terms[: WINDOW - 8, :HALF] + terms[8:, HALF:]
        for shift in (4, 2, 1):
            up = pltpu.roll(part, WINDOW - 8 - shift, 0)
            part = jnp.where(lane & (GROUP * shift) != 0, up, part)
        return part[:FREQ]

    parts, ahead = [], raw(places[0])
    for place in places[1:]:
        terms, ahead = ahead, raw(place)
        parts.append(aligned(terms))
    parts.append(aligned(ahead))
    lane = lax.broadcasted_iota(jnp.int32, (FREQ, HALF), 1)

    def merged(first, second, width):
        low = lane & width == 0
        rest = jnp.where(low, second, first)
        rest = pltpu.roll(rest, width, 1) if width == HALF // 2 else exchanged(rest, lane, width)
        return jnp.where(low, first, second) + rest

    both = merged(merged(parts[0], parts[2], 64), merged(parts[1], parts[3], 64), 32)
    return both + exchanged(both, lane, 16)


def interleaved(even, odd):
    lane = lax.broadcasted_iota(jnp.int32, (FREQ, HALF), 1)
    return jnp.where(lane & GROUP == 0, even, odd)


def by_owner(total):
    flipped = total.T.reshape(HALF // 8, 8, FREQ)
    return jnp.concatenate([flipped[:, :, :HALF], flipped[:, :, HALF:]], axis=1)


def first_kernel(core, far, near, own, shifts, win, even, ext):
    windows(core[0], near, far, own, ext, win)
    even[...] = lags(win, shifts, 1 - core[0], EVEN)


def second_kernel(core, win, shifts, even, out, kept):
    out[...] = by_owner(interleaved(even[...], lags(win, shifts, 1 - core[0], ODD)))
    kept[...] = lags(win, shifts, core[0], EVEN)


def third_kernel(core, win, shifts, kept, keep_z, out):
    out[:, :16] = by_owner(interleaved(kept[...], lags(win, shifts, core[0], ODD)))
    out[:, 16:] = keep_z[...]


def cos_sin(theta):
    turns = jnp.round(theta * (2 / np.pi))
    rest = theta - turns * 1.5703125
    rest = rest - turns * 4.837512969970703e-4
    rest = rest - turns * 7.549789948768648e-8
    square = rest * rest
    sin = rest + rest * square * (
        -1.6666654611e-1 + square * (8.3321608736e-3 + square * -1.9515295891e-4)
    )
    cos = (1.0 - 0.5 * square) + square * square * (
        4.166664568298827e-2 + square * (-1.388731625493765e-3 + square * 2.443315711809948e-5)
    )
    quarter = turns.astype(jnp.int32)
    odd = quarter & 1 != 0
    real, imag = jnp.where(odd, sin, cos), jnp.where(odd, cos, sin)
    real = jnp.where((quarter + 1) & 2 != 0, -real, real)
    imag = jnp.where(quarter & 2 != 0, -imag, imag)
    return real, imag


def field_kernel(
    first, depth, core, defocus, phase, send_k, high, low, keep, send, field_re, field_im, ordered
):
    blocks, rows, width = phase.shape
    for block in range(blocks):
        ordered[depth[0] ^ GATHER_MASKS[block]] = phase[block]
    full = jnp.concatenate([ordered[block] for block in range(blocks)], axis=1)
    centre = (PUPIL - 1) / 2.0
    shape = (rows, PUPIL)
    u = (lax.broadcasted_iota(jnp.int32, shape, 0) + first[0]).astype(jnp.float32)
    v = lax.broadcasted_iota(jnp.int32, shape, 1).astype(jnp.float32)
    radius = (u - centre) ** 2 + (v - centre) ** 2
    limit = (PUPIL / 2.0) ** 2
    inside = radius <= limit
    real, imag = cos_sin(full + defocus[0].astype(jnp.float32) * defocus_step * (radius / limit))
    real, imag = jnp.where(inside, real, 0.0), jnp.where(inside, imag, 0.0)
    field_re[...] = real
    field_im[...] = imag
    terms = dot3(jnp.concatenate([real, imag], axis=0), high, low)
    z_re = terms[:rows, :FREQ] - terms[rows:, FREQ:]
    z_im = terms[:rows, FREQ:] + terms[rows:, :FREQ]
    here = core[0] == 0
    blank = jnp.zeros((rows, FREQ), jnp.float32)
    first_re, second_re = jnp.where(here, z_re, blank), jnp.where(here, blank, z_re)
    first_im, second_im = jnp.where(here, z_im, blank), jnp.where(here, blank, z_im)
    z = jnp.concatenate([first_re, second_re, first_im, second_im], axis=0).T
    z_low, z_high = z[:HALF], z[HALF:]
    keep[...] = jnp.where(here, z_low, z_high).reshape(keep.shape)
    send[:, :16] = send_k[...]
    send[:, 16:] = jnp.where(here, z_high, z_low).reshape(keep.shape)


def middle_kernel(payload, g_high, g_low, s_high, s_low, out):
    chips = payload.shape[0]
    rows = PUPIL // chips
    kernel_grad = payload[0, :16]
    for chip in range(1, chips):
        kernel_grad = kernel_grad + payload[chip, :16]
    kernel_grad = jnp.concatenate([kernel_grad[:8], kernel_grad[8:]], axis=1)
    order = [CHIP_ORDER.index(chip) for chip in range(chips)]
    z_re = jnp.concatenate([payload[place, 16:, :rows] for place in order], axis=1)
    z_im = jnp.concatenate([payload[place, 16:, rows:] for place in order], axis=1)
    terms = dot3(jnp.concatenate([z_re, z_im], axis=0), g_high, g_low)
    y_re = terms[:8, :FREQ] - terms[8:, FREQ:]
    y_im = terms[:8, FREQ:] + terms[8:, :FREQ]
    gy = 2.0 * jnp.concatenate([kernel_grad * y_re, kernel_grad * y_im], axis=0)
    terms = dot3(gy, s_high, s_low)
    gz_re = terms[:8, :PUPIL] + terms[8:, PUPIL:]
    gz_im = terms[8:, :PUPIL] - terms[:8, PUPIL:]
    rows = rows // 2
    for tile in range(2 * chips):
        here = slice(rows * tile, rows * (tile + 1))
        parts = [part[:, here] for part in (gz_re, gz_im)]
        rows_of = [part[half : half + 4] for half in (0, 4) for part in parts]
        out[TILE_ORDER.index(tile)] = jnp.concatenate(rows_of, axis=1)


def phase_kernel(payload, field_re, field_im, high, low, out):
    rows = field_re.shape[0]
    gz = payload[...].T
    gz_re = jnp.concatenate([gz[:rows], gz[2 * rows : 3 * rows]], axis=1)
    gz_im = jnp.concatenate([gz[rows : 2 * rows], gz[3 * rows :]], axis=1)
    terms = dot3(jnp.concatenate([gz_re, gz_im], axis=0), high, low)
    ge_re = terms[:rows, :PUPIL] + terms[rows:, PUPIL:]
    ge_im = terms[rows:, :PUPIL] - terms[:rows, PUPIL:]
    phase = field_re[...] * ge_im - field_im[...] * ge_re
    width = out.shape[2]
    for block in range(out.shape[0]):
        out[DEPTH_ORDER.index(block)] = phase[:, width * block : width * (block + 1)]


def call(kernel, outs, scratch, flops, moved, smem=0):
    def run(*args):
        spaces = [pltpu.SMEM if place < smem else pltpu.VMEM for place in range(len(args))]
        return pl.pallas_call(
            kernel,
            out_shape=outs,
            in_specs=[pl.BlockSpec(memory_space=space) for space in spaces],
            out_specs=jax.tree.map(lambda _: pl.BlockSpec(memory_space=pltpu.VMEM), outs),
            scratch_shapes=scratch,
            compiler_params=pltpu.CompilerParams(vmem_limit_bytes=40 * 2**20),
            cost_estimate=pl.CostEstimate(flops=flops, bytes_accessed=moved, transcendentals=0),
        )(*args)

    return run


def over_depth(x, mask):
    count = lax.axis_size("depth")
    return lax.ppermute(x, "depth", [(i, i ^ mask) for i in range(count)])


def beside(x, tiles):
    pairs = [(i, i + 1) for i in range(1, tiles - 1, 2)]
    return lax.ppermute(x, ("chip", "core"), pairs + [(j, i) for i, j in pairs])


def redistribute(x, axis, order):
    return lax.all_to_all(x, axis, 0, 0, tiled=True, axis_index_groups=[list(order)])


def swap(x):
    return lax.ppermute(x, "core", [(0, 1), (1, 0)])


def body(scene_layers, sensor_grad, pupil_phase, defocus_index):
    chips, depths = lax.axis_size("chip"), lax.axis_size("depth")
    rows, width = pupil_phase.shape
    f32 = jnp.float32
    (g_high, g_low), (s_high, s_low), (r_high, r_low) = freq_tables()
    core, depth, first_row = (
        lax.axis_index(axis).astype(jnp.int32)[None] for axis in ("core", "depth", ("chip", "core"))
    )
    first_row = first_row * rows
    scene = scene_layers[0]
    steps = scene.shape[0] // GROUP
    work = 2 * steps * FREQ * WINDOW * FREQ
    far = beside(scene, 2 * chips)
    other = over_depth(pupil_phase, GATHER_MASKS[1])
    shape, bf16 = jax.ShapeDtypeStruct, jnp.bfloat16
    shifts = call(
        shift_kernel,
        shape((steps, 2 * FREQ, FREQ), bf16),
        [],
        2 * scene.shape[0] * FREQ * FREQ * GROUP,
        2**22,
    )(sensor_grad)
    other, shifts, edge = lax.optimization_barrier((other, shifts, scene))
    near = swap(edge)
    gathered = jnp.stack([pupil_phase, other])
    beyond = over_depth(gathered, GATHER_MASKS[2])
    far, near, shifts = lax.optimization_barrier((far, near, shifts))
    lanes = shape((FREQ, HALF), f32)
    win, even = call(
        first_kernel,
        (shape((WINDOW, steps * FREQ), bf16), lanes),
        [pltpu.VMEM((3 * scene.shape[0], FREQ), bf16)],
        4 * work,
        2**19,
        smem=1,
    )(core, far, near, scene, shifts)
    beyond, win, even = lax.optimization_barrier((beyond, win, even))
    gathered = jnp.concatenate([gathered, beyond], axis=0)
    beyond = over_depth(gathered, GATHER_MASKS[4])
    send_k, even = call(
        second_kernel, (shape((chips, 16, HALF), f32), lanes), [], 8 * work, 2**19, smem=1
    )(core, win, shifts, even)
    beyond, send_k, even = lax.optimization_barrier((beyond, send_k, even))
    gathered = jnp.concatenate([gathered, beyond], axis=0)
    piece, both = shape((chips, 8, HALF), f32), shape((chips, 24, HALF), f32)
    field = shape((rows, PUPIL), f32)
    keep_z, send, field_re, field_im = call(
        field_kernel,
        (piece, both, field, field),
        [pltpu.VMEM((depths, rows, width), f32)],
        2 * 192 * PUPIL * 2 * FREQ,
        3 * 2**20,
        smem=4,
    )(first_row, depth, core, defocus_index, gathered, send_k, g_high, g_low)
    send, win = lax.optimization_barrier((send, win))
    other = swap(send)
    keep = call(third_kernel, both, [], 4 * work, 2**19, smem=1)(core, win, shifts, even, keep_z)
    other, keep = lax.optimization_barrier((other, keep))
    payload = redistribute(keep + other, "chip", CHIP_ORDER)
    payload = call(
        middle_kernel,
        jax.ShapeDtypeStruct((2 * chips, 4, HALF), f32),
        [],
        2 * 96 * PUPIL * 2 * FREQ,
        5 * 2**20,
    )(payload, g_high, g_low, s_high, s_low)
    payload = redistribute(payload, ("chip", "core"), TILE_ORDER)
    parts = call(
        phase_kernel,
        jax.ShapeDtypeStruct((depths, rows, width), f32),
        [],
        2 * 192 * PUPIL * 2 * FREQ,
        3 * 2**20,
    )(payload.reshape(HALF, HALF), field_re, field_im, r_high, r_low)
    parts = redistribute(parts, "depth", DEPTH_ORDER)
    return jnp.sum(parts, axis=0)


def solution(mesh):
    depths, tiles = mesh.devices.shape
    split_mesh = jax.sharding.Mesh(
        mesh.devices.reshape(depths, tiles // 2, 2), ("depth", "chip", "core")
    )
    rows = ("chip", "core")
    placed = (P("depth", rows, None), P(rows, None), P(rows, "depth"), P("depth"))
    return jax.shard_map(
        body, mesh=split_mesh, in_specs=placed, out_specs=P(rows, "depth"), check_vma=False
    )
```
